32 devices in a mesh: mem: 4 (over y, x), tok: 8 (over z, core).
Axes of the slice: x: 2, y: 2, z: 4, core: 2. Of those that a mesh axis runs over, the one named last changes fastest.
Arguments:
- queries: bfloat16 [8192, 4096], P('tok', 'mem'), may hold values from -6 to 6
- keys: bfloat16 [8192, 4096], P('tok', 'mem'), may hold values from -6 to 6
- values: bfloat16 [8192, 4096], P('tok', 'mem'), may hold values from -6 to 6
- memory: bfloat16 [32, 128, 128, 256], P('mem', 'tok'), may hold values from -6 to 6
- block_ids: int32 [16, 32, 4], P('tok', 'mem'), may hold values from 0 to 127, as said below
- gate_bias: float32 [32], P('mem'), may hold values from -2 to 2
- grad_out: bfloat16 [8192, 4096], P('tok', 'mem'), may hold values from -6 to 6
Outputs:
- output: bfloat16 [8192, 4096], P('tok', 'mem')
- grad_queries: bfloat16 [8192, 4096], P('tok', 'mem')
- grad_keys: bfloat16 [8192, 4096], P('tok', 'mem')
- grad_values: bfloat16 [8192, 4096], P('tok', 'mem')
The draws below stay inside these ranges and needn't reach their ends.
Inputs may be any that keep to these rules, and one draw needn't show every extreme that they name: `block_ids`: within one span and head the 4 ids differ. The ids held by one device (2 spans, 8 heads) name at most 16 blocks of any one memory shard (id // 16); in every draw some shard is named exactly 16 times by every such device.
All inputs are finite; a program needn't handle non-finite values.
Results may differ from the reference program's by a relative error of at most 0.02.
Values may be sent and summed in bfloat16 or wider, within the bound.
No kernel may reach another device: no remote copies, remote signals or barrier semaphores. Data moves between devices by JAX's collectives and lax.ppermute only.
A program may use at most 128 MiB of HBM per device.

```python
import jax
import jax.numpy as jnp
from jax import lax

H = 32
HD = 128
SPAN_TOKENS = 512
BLOCK = 128
R = 4
SPAN_DEV = 2
NB_DEV = 16
HL = 8
CAP = 16
SPANS = 16
TOKENS = 8192
NB = 128


def token_field(key):
    shape = (TOKENS, H * HD)
    field = jnp.clip(jax.random.normal(key, shape, jnp.float32), -5.0, 5.0)
    return field.astype(jnp.bfloat16)


def draw_queries(key, part):
    return token_field(jax.random.fold_in(key, 31))


def draw_keys(key, part):
    inner = jax.random.fold_in(key, 32)
    return token_field(inner)


def draw_memory(key, part):
    inner = jax.random.fold_in(key, 33)
    field = jnp.clip(jax.random.normal(inner, (H, NB, BLOCK, 2 * HD), jnp.float32), -5.0, 5.0)
    return field.astype(jnp.bfloat16)


def draw_block_ids(key, part):
    tok_count = SPANS // SPAN_DEV
    mem_count = H // HL
    request_count = SPAN_DEV * HL * R
    slot_total = tok_count * CAP
    hot_owner = jax.random.randint(jax.random.fold_in(key, 11), (), 0, tok_count)
    slot_owner = jnp.arange(slot_total) // CAP

    def one_group(group_key):
        first_key, second_key, third_key = jax.random.split(group_key, 3)
        shuffled = slot_owner[jax.random.permutation(first_key, slot_total)]
        priority = jnp.where(shuffled == hot_owner, 0, 1 + jnp.arange(slot_total))
        chosen = shuffled[jnp.argsort(priority, stable=True)][:request_count]
        chosen = chosen[jax.random.permutation(second_key, request_count)]
        owners = chosen.reshape(SPAN_DEV * HL, R)
        same_owner = owners[:, :, None] == owners[:, None, :]
        rank_ids = jnp.arange(R)
        earlier = jnp.sum(same_owner & (rank_ids[None, None, :] < rank_ids[None, :, None]), axis=2)
        first_seen = jnp.min(jnp.where(same_owner, rank_ids[None, None, :], R), axis=2)
        offsets = jax.random.randint(third_key, (SPAN_DEV * HL, R), 0, NB_DEV)
        base_offset = jnp.take_along_axis(offsets, first_seen, axis=1)
        local_index = (base_offset + earlier) % NB_DEV
        return (owners * NB_DEV + local_index).reshape(SPAN_DEV, HL, R)
    group_keys = jax.random.split(jax.random.fold_in(key, 12), tok_count * mem_count)
    grouped = jax.vmap(one_group)(group_keys).reshape(tok_count, mem_count, SPAN_DEV, HL, R)
    return grouped.transpose(0, 2, 1, 3, 4).reshape(SPANS, H, R).astype(jnp.int32)


def block_levels(rng, dims, shards, least, largest):
    factor_of, own = 1.0, jax.random.fold_in(rng, 6)
    for axis_at, parts in shards:
        heights = jnp.exp(jax.random.uniform(jax.random.fold_in(own, axis_at), (parts,), jnp.float32, least / len(shards), largest / len(shards)))
        factor_of = factor_of * jnp.repeat(heights, dims[axis_at] // parts).reshape([-1 if axis == axis_at else 1 for axis in range(len(dims))])
    return factor_of


def gaussian(rng, dims, deviation, reach, pieces=(), held_as=jnp.bfloat16):
    values = jax.random.normal(rng, dims, jnp.float32) * deviation
    if len(pieces) > 0:
        values = block_levels(rng, dims, pieces, -0.22, 0.18) * values
    return jnp.clip(values, min=-reach, max=reach).astype(held_as)


def setup_inputs(seed: int = 0) -> dict:
    splits = jax.random.split(jax.random.key(seed), 8)
    queries = draw_queries(jax.random.fold_in(splits[7], 71), 0)
    keys = draw_keys(jax.random.fold_in(splits[7], 71), 0)
    values = gaussian(splits[2], (TOKENS, H * HD), 1.0, 6.0, ((0, 8), (1, 4)))
    memory = draw_memory(jax.random.fold_in(splits[7], 71), 0)
    block_ids = draw_block_ids(jax.random.fold_in(splits[7], 71), 0)
    gate_bias = jnp.clip(jax.random.uniform(splits[5], (H,), jnp.float32, -2.0, 2.0) * block_levels(splits[5], (H,), ((0, 4),), -0.4, 0.0), -2.0, 2.0)
    grad_out = gaussian(splits[6], (TOKENS, H * HD), 1.0, 6.0, ((0, 8), (1, 4)))
    return {"queries": queries, "keys": keys, "values": values, "memory": memory, "block_ids": block_ids, "gate_bias": gate_bias, "grad_out": grad_out}


def head_pass(query, keys_ext, values_ext, mem_keys, mem_values, grad_rows, gate_value, prev_ok):
    length = query.shape[0]
    scaling = query.shape[1] ** -0.5
    row_ids = jnp.arange(length)[:, None]
    col_ids = jnp.arange(2 * length)[None, :]
    allowed = (col_ids <= row_ids + length) & ((col_ids >= length) | prev_ok)
    scores = jnp.dot(query, keys_ext.T, preferred_element_type=jnp.float32) * scaling
    scores = jnp.where(allowed, scores, -jnp.inf)
    row_max = jnp.max(scores, axis=1, keepdims=True)
    weights = jnp.where(allowed, jnp.exp(scores - row_max), 0.0)
    row_sum = jnp.sum(weights, axis=1, keepdims=True)
    attention_weights = (weights / row_sum).astype(jnp.bfloat16)
    local_out = jnp.dot(attention_weights, values_ext, preferred_element_type=jnp.float32)
    mem_scores = jnp.dot(query, mem_keys.T, preferred_element_type=jnp.float32) * scaling
    mem_max = jnp.max(mem_scores, axis=1, keepdims=True)
    mem_weights = jnp.exp(mem_scores - mem_max)
    mem_probs = (mem_weights / jnp.sum(mem_weights, axis=1, keepdims=True)).astype(jnp.bfloat16)
    mem_out = jnp.dot(mem_probs, mem_values, preferred_element_type=jnp.float32)
    output = gate_value * mem_out + (1.0 - gate_value) * local_out
    grad_float = grad_rows.astype(jnp.float32)
    local_gradient = ((1.0 - gate_value) * grad_float).astype(jnp.bfloat16)
    grad_mem = (gate_value * grad_float).astype(jnp.bfloat16)
    local_dprobs = jnp.dot(local_gradient, values_ext.T, preferred_element_type=jnp.float32)
    extended_value_gradient = jnp.dot(attention_weights.T, local_gradient, preferred_element_type=jnp.float32)
    probs_float = attention_weights.astype(jnp.float32)
    row_dot = jnp.sum(probs_float * local_dprobs, axis=1, keepdims=True)
    local_dscores = (probs_float * (local_dprobs - row_dot) * scaling).astype(jnp.bfloat16)
    query_gradient = jnp.dot(local_dscores, keys_ext, preferred_element_type=jnp.float32)
    extended_key_gradient = jnp.dot(local_dscores.T, query, preferred_element_type=jnp.float32)
    mem_dprobs = jnp.dot(grad_mem, mem_values.T, preferred_element_type=jnp.float32)
    mem_float = mem_probs.astype(jnp.float32)
    mem_dot = jnp.sum(mem_float * mem_dprobs, axis=1, keepdims=True)
    mem_dscores = (mem_float * (mem_dprobs - mem_dot) * scaling).astype(jnp.bfloat16)
    query_gradient = query_gradient + jnp.dot(mem_dscores, mem_keys, preferred_element_type=jnp.float32)
    return (output.astype(jnp.bfloat16), query_gradient.astype(jnp.bfloat16), extended_key_gradient, extended_value_gradient,
            row_max[:, 0], row_sum[:, 0], row_dot[:, 0])


def span_sweep(query, keys_ext, values_ext, blocks, grad_rows, gates, prev_ok):
    head_count = gates.shape[0]
    head_size = blocks.shape[-1] // 2

    def split_heads(matrix):
        return matrix.reshape(matrix.shape[0], head_count, head_size).transpose(1, 0, 2)

    def join_heads(stacked):
        return stacked.transpose(1, 0, 2).reshape(stacked.shape[1], head_count * head_size)

    mem_keys = blocks[..., :head_size].reshape(head_count, -1, head_size)
    mem_values = blocks[..., head_size:].reshape(head_count, -1, head_size)

    def per_head(inputs):
        return head_pass(inputs[0], inputs[1], inputs[2], inputs[3], inputs[4], inputs[5], inputs[6], prev_ok)

    result = lax.map(per_head, (split_heads(query), split_heads(keys_ext), split_heads(values_ext),
                                mem_keys, mem_values, split_heads(grad_rows), gates))
    return (join_heads(result[0]), join_heads(result[1]), join_heads(result[2]), join_heads(result[3]),
            (result[4], result[5], result[6]))


def reference(queries, keys, values, memory, block_ids, gate_bias, grad_out):
    gates = jax.nn.sigmoid(gate_bias)
    width = H * HD
    zero_rows = jnp.zeros((SPAN_TOKENS, width), keys.dtype)
    keys_pad = jnp.concatenate([zero_rows, keys], axis=0)
    values_pad = jnp.concatenate([zero_rows, values], axis=0)
    head_rows = jnp.arange(H)[:, None]

    def step(running_state, index):
        start = (index * SPAN_TOKENS).astype(jnp.int32)
        query = lax.dynamic_slice_in_dim(queries, start, SPAN_TOKENS, 0)
        grad_rows = lax.dynamic_slice_in_dim(grad_out, start, SPAN_TOKENS, 0)
        keys_ext = lax.dynamic_slice_in_dim(keys_pad, start, 2 * SPAN_TOKENS, 0)
        values_ext = lax.dynamic_slice_in_dim(values_pad, start, 2 * SPAN_TOKENS, 0)
        picked = memory[head_rows, block_ids[index]]
        output, query_gradient, extended_key_gradient, extended_value_gradient, softmax_totals = span_sweep(
            query, keys_ext, values_ext, picked, grad_rows, gates, index > 0)
        key_gradient = (extended_key_gradient[SPAN_TOKENS:] + running_state[0]).astype(jnp.bfloat16)
        value_gradient = (extended_value_gradient[SPAN_TOKENS:] + running_state[1]).astype(jnp.bfloat16)
        return (extended_key_gradient[:SPAN_TOKENS], extended_value_gradient[:SPAN_TOKENS]), (output, query_gradient, key_gradient, value_gradient)

    start_carry = (jnp.zeros((SPAN_TOKENS, width), jnp.float32), jnp.zeros((SPAN_TOKENS, width), jnp.float32))
    final_carry, stacked = lax.scan(step, start_carry, jnp.arange(SPANS, dtype=jnp.int32), reverse=True)
    return (stacked[0].reshape(TOKENS, width), stacked[1].reshape(TOKENS, width),
            stacked[2].reshape(TOKENS, width), stacked[3].reshape(TOKENS, width))
```

```python
import functools

import jax
import jax.numpy as jnp
from jax import lax
from jax.experimental import pallas as pl
from jax.experimental.pallas import tpu as pltpu
from jax.sharding import PartitionSpec as P

SPAN = 512
HALF = 256
BLOCK = 128
R = 4
HD = 128
NEG = -1e30
ANY = pl.BlockSpec(memory_space=pl.ANY)
SMEM = pl.BlockSpec(memory_space=pltpu.SMEM)


def passed_along(block, axis, distance):
    devices = range(lax.axis_size(axis))
    route = [(i - distance, i) for i in devices if i - distance in devices]
    return lax.ppermute(block, axis, route)


def mm(a, b, dims):
    return lax.dot_general(a, b, (dims, ((), ())), preferred_element_type=jnp.float32)


def local_kernel(head, n_any, gates, prev_ok, q_ref, k_ref, v_ref, g_ref, hk_ref, hv_ref, *rest):
    (lo_ref, dq_ref, dk_ref, dv_ref, dkx_ref, dvx_ref, hdk_ref, hdv_ref, token_ref,
     kx, vx, kt, vt, acc_k, acc_v) = rest[n_any:]
    scaling = HD ** -0.5
    keep = 1.0 - gates[head]
    kx[:SPAN] = hk_ref[...]
    kx[SPAN:] = k_ref[...]
    vx[:SPAN] = hv_ref[...]
    vx[SPAN:] = v_ref[...]
    kt[...] = kx[...].T
    vt[...] = vx[...].T
    ok = prev_ok[0] > 0
    tri = (lax.broadcasted_iota(jnp.int32, (HALF, HALF), 0)
           <= lax.broadcasted_iota(jnp.int32, (HALF, HALF), 1))
    for span in range(2):
        for half in range(2):
            row0 = span * SPAN + half * HALF
            win0 = span * SPAN
            width = SPAN + HALF * (half + 1)
            rows = pl.ds(row0, HALF)
            win = pl.ds(win0, width)
            q = q_ref[rows, :]
            gl = (keep * g_ref[rows, :].astype(jnp.float32)).astype(jnp.bfloat16)
            st = mm(kx[win, :], q, ((1,), (1,))) * scaling
            first = st[:SPAN]
            if span == 0:
                first = jnp.where(ok, first, NEG)
            parts = [first]
            if half:
                parts.append(st[SPAN:width - HALF])
            parts.append(jnp.where(tri, st[width - HALF:], NEG))
            st = jnp.concatenate(parts, axis=0)
            top = jnp.max(st, axis=0, keepdims=True)
            e = jnp.exp(st - top)
            total = jnp.sum(e, axis=0, keepdims=True)
            pt = (e * (1.0 / total)).astype(jnp.bfloat16)
            out_t = mm(vt[:, win], pt, ((1,), (0,)))
            gt = gl.astype(jnp.float32).T
            dot = jnp.sum(gt * out_t, axis=0, keepdims=True)
            dpt = mm(vx[win, :], gl, ((1,), (1,)))
            dst = (pt.astype(jnp.float32) * (dpt - dot)).astype(jnp.bfloat16)
            dq_t = mm(kt[:, win], dst, ((1,), (0,)))
            lo_ref[rows, :] = keep * out_t.T
            dq_ref[rows, :] = scaling * dq_t.T
            dkw = mm(dst, q, ((1,), (0,)))
            dvw = mm(pt, gl, ((1,), (0,)))
            if span == 0 and half == 0:
                acc_k[win, :] = dkw
                acc_v[win, :] = dvw
            else:
                old = 768 if span == 0 else (1024 if half == 0 else 1280)
                seen = max(0, min(old, win0 + width) - win0)
                acc_k[pl.ds(win0, seen), :] += dkw[:seen]
                acc_v[pl.ds(win0, seen), :] += dvw[:seen]
                if seen < width:
                    acc_k[pl.ds(win0 + seen, width - seen), :] = dkw[seen:]
                    acc_v[pl.ds(win0 + seen, width - seen), :] = dvw[seen:]
    hdk_ref[...] = (scaling * acc_k[:SPAN]).astype(jnp.bfloat16)
    hdv_ref[...] = acc_v[:SPAN].astype(jnp.bfloat16)
    dk_ref[...] = (scaling * acc_k[SPAN:2 * SPAN]).astype(jnp.bfloat16)
    dv_ref[...] = acc_v[SPAN:2 * SPAN].astype(jnp.bfloat16)
    dkx_ref[...] = scaling * acc_k[2 * SPAN:]
    dvx_ref[...] = acc_v[2 * SPAN:]
    token_ref[...] = jnp.zeros_like(token_ref)


def local_head(head, gates, prev_ok, q, k, v, g, hk, hv, carry, after):
    rows, width = q.shape
    col = pl.BlockSpec((rows, HD), lambda i: (0, head))
    col_half = pl.BlockSpec((SPAN, HD), lambda i: (0, head))
    alone = pl.BlockSpec((SPAN, HD), lambda i: (0, 0))
    shapes = [
        jax.ShapeDtypeStruct((rows, width), jnp.float32),
        jax.ShapeDtypeStruct((rows, width), jnp.float32),
        jax.ShapeDtypeStruct((rows, width), jnp.bfloat16),
        jax.ShapeDtypeStruct((rows, width), jnp.bfloat16),
        jax.ShapeDtypeStruct((SPAN, width), jnp.float32),
        jax.ShapeDtypeStruct((SPAN, width), jnp.float32),
        jax.ShapeDtypeStruct((SPAN, HD), jnp.bfloat16),
        jax.ShapeDtypeStruct((SPAN, HD), jnp.bfloat16),
        jax.ShapeDtypeStruct((8, 128), jnp.float32),
    ]
    extra = list(carry) + list(after)
    result = pl.pallas_call(
        functools.partial(local_kernel, head, len(extra)),
        grid=(1,),
        out_shape=shapes,
        in_specs=[SMEM, SMEM, col, col, col, col, col_half, col_half] + [ANY] * len(extra),
        out_specs=[col, col, col_half, col_half, col_half, col_half, alone, alone,
                   pl.BlockSpec((8, 128), lambda i: (0, 0))],
        scratch_shapes=[
            pltpu.VMEM((3 * SPAN, HD), jnp.bfloat16),
            pltpu.VMEM((3 * SPAN, HD), jnp.bfloat16),
            pltpu.VMEM((HD, 3 * SPAN), jnp.bfloat16),
            pltpu.VMEM((HD, 3 * SPAN), jnp.bfloat16),
            pltpu.VMEM((3 * SPAN, HD), jnp.float32),
            pltpu.VMEM((3 * SPAN, HD), jnp.float32),
        ],
        input_output_aliases={8 + i: i for i in range(len(carry))},
        compiler_params=pltpu.CompilerParams(vmem_limit_bytes=32 * 2**20),
        cost_estimate=pl.CostEstimate(flops=6 * 2 * 2 * 512 * 896 * 128, bytes_accessed=4 * 2**20,
                                      transcendentals=2 * 512 * 896),
        name="local_head",
    )(gates, prev_ok, q, k, v, g, hk, hv, *extra)
    return result[:6], result[6], result[7], result[8]


def memory_kernel(counts, loc, gates, q_ref, g_ref, lo_ref, dqf_ref, dkx_ref, dvx_ref, ink_ref,
                  inv_ref, near, sib, pool, dk_in, dv_in, out_ref, dq_ref, dk_ref, dv_ref, buf,
                  sems):
    n_near, n_sib = counts
    head = pl.program_id(0)
    heads = pl.num_programs(0)
    scaling = HD ** -0.5

    def fetch(h, slot):
        for j in range(2 * R):
            index = loc[j // R, h, j % R]
            place = buf.at[slot, j]
            sem = sems.at[slot, j]

            @pl.when(index < n_near)
            def _():
                pltpu.make_async_copy(near.at[index], place, sem).start()

            @pl.when((index >= n_near) & (index < n_near + n_sib))
            def _():
                pltpu.make_async_copy(sib.at[index - n_near], place, sem).start()

            @pl.when(index >= n_near + n_sib)
            def _():
                pltpu.make_async_copy(pool.at[index - n_near - n_sib], place, sem).start()

    slot = lax.rem(head, 2)

    @pl.when(head == 0)
    def _():
        fetch(0, 0)

    @pl.when(head + 1 < heads)
    def _():
        fetch(head + 1, 1 - slot)

    dk_ref[...] = (dkx_ref[...] + ink_ref[...].astype(jnp.float32)).astype(jnp.bfloat16)
    dv_ref[...] = (dvx_ref[...] + inv_ref[...].astype(jnp.float32)).astype(jnp.bfloat16)
    for j in range(2 * R):
        pltpu.make_async_copy(near.at[0], buf.at[slot, j], sems.at[slot, j]).wait()
    gate = gates[head]
    for span in range(2):
        blocks = buf[slot, pl.ds(span * R, R)]
        mk = blocks[:, :, :HD].reshape(R * BLOCK, HD)
        mv = blocks[:, :, HD:].reshape(R * BLOCK, HD)
        for half in range(2):
            rows = pl.ds(span * SPAN + half * HALF, HALF)
            q = q_ref[rows, :]
            gm = (gate * g_ref[rows, :].astype(jnp.float32)).astype(jnp.bfloat16)
            s = mm(q, mk, ((1,), (1,))) * scaling
            top = jnp.max(s, axis=1, keepdims=True)
            e = jnp.exp(s - top)
            total = jnp.sum(e, axis=1, keepdims=True)
            p = (e * (1.0 / total)).astype(jnp.bfloat16)
            mo = mm(p, mv, ((1,), (0,)))
            dp = mm(gm, mv, ((1,), (1,)))
            dot = jnp.sum(gm.astype(jnp.float32) * mo, axis=1, keepdims=True)
            ds = (p.astype(jnp.float32) * (dp - dot)).astype(jnp.bfloat16)
            dqm = mm(ds, mk, ((1,), (0,)))
            out_ref[rows, :] = (gate * mo + lo_ref[rows, :]).astype(jnp.bfloat16)
            dq_ref[rows, :] = (scaling * dqm + dqf_ref[rows, :]).astype(jnp.bfloat16)


def memory_heads(loc, gates, q, g, carry, ink, inv, near, sib, pool):
    lo, dqf, dk, dv, dkx, dvx = carry
    rows, width = q.shape
    heads = width // HD
    col = pl.BlockSpec((rows, HD), lambda h: (0, h))
    col_half = pl.BlockSpec((SPAN, HD), lambda h: (0, h))
    lower = pl.BlockSpec((SPAN, HD), lambda h: (1, h))
    full = jax.ShapeDtypeStruct((rows, width), jnp.bfloat16)
    return pl.pallas_call(
        functools.partial(memory_kernel, (near.shape[0], sib.shape[0])),
        grid=(heads,),
        out_shape=[full] * 4,
        in_specs=[SMEM, SMEM, col, col, col, col, col_half, col_half, col_half, col_half]
        + [ANY] * 5,
        out_specs=[col, col, lower, lower],
        scratch_shapes=[
            pltpu.VMEM((2, 2 * R, BLOCK, 2 * HD), jnp.bfloat16),
            pltpu.SemaphoreType.DMA((2, 2 * R)),
        ],
        input_output_aliases={13: 2, 14: 3},
        compiler_params=pltpu.CompilerParams(vmem_limit_bytes=32 * 2**20),
        cost_estimate=pl.CostEstimate(flops=heads * 4 * 2 * 2 * 512 * 512 * 128,
                                      bytes_accessed=24 * 2**20,
                                      transcendentals=heads * 2 * 512 * 512),
        name="memory_heads",
    )(loc, gates, q, g, lo, dqf, dkx, dvx, ink, inv, near, sib, pool, dk, dv)


def exchange_all(memory, block_ids):
    tok_count = lax.axis_size("tok")
    heads_here, blocks_here = memory.shape[:2]
    wanted = block_ids.reshape(-1)
    request_count = wanted.shape[0]
    owner_rank = wanted // blocks_here
    head_index = jnp.arange(request_count) // R % heads_here
    request_code = head_index * blocks_here + wanted % blocks_here
    order_ids = jnp.arange(request_count)
    same_owner = owner_rank[:, None] == owner_rank[None, :]
    slot_index = jnp.sum(same_owner & (order_ids[None, :] < order_ids[:, None]), axis=1)
    capacity = 2 * request_count // tok_count
    to_owner = (owner_rank[:, None] == jnp.arange(tok_count)[None, :]).astype(jnp.int32)
    to_slot = (slot_index[:, None] == jnp.arange(capacity)[None, :]).astype(jnp.int32)
    request_table = jnp.sum(
        request_code[:, None, None] * to_owner[:, :, None] * to_slot[:, None, :], axis=0
    )
    mem_flat = memory.reshape(-1, BLOCK, memory.shape[-1])
    found = mem_flat[lax.all_to_all(request_table, "tok", split_axis=0, concat_axis=0, tiled=True)]
    returned = lax.all_to_all(found, "tok", split_axis=0, concat_axis=0, tiled=True)
    loc = (owner_rank * capacity + slot_index).reshape(block_ids.shape)
    return returned.reshape(-1, BLOCK, memory.shape[-1]), loc.astype(jnp.int32)


def per_device(queries, keys, values, memory, block_ids, gate_bias, grad_out):
    my_rank = lax.axis_index("tok")
    heads = gate_bias.shape[0]
    gates = jax.nn.sigmoid(gate_bias)
    prev_ok = (my_rank > 0).astype(jnp.int32).reshape(1)
    hk = passed_along(keys[-SPAN:], "tok", 1)
    hv = passed_along(values[-SPAN:], "tok", 1)
    returned, loc = exchange_all(memory, block_ids)
    carry, token = (), ()
    halo_k, halo_v = [], []
    for head in range(heads):
        carry, dk, dv, token = local_head(
            head, gates, prev_ok, queries, keys, values, grad_out, hk, hv, carry, token
        )
        token = (token,)
        halo_k.append(dk)
        halo_v.append(dv)
    ink = passed_along(jnp.concatenate(halo_k, axis=1), "tok", -1)
    inv = passed_along(jnp.concatenate(halo_v, axis=1), "tok", -1)
    return tuple(
        memory_heads(loc, gates, queries, grad_out, carry, ink, inv, returned, returned, returned)
    )


def solution(mesh):
    in_specs = (
        P("tok", "mem"),
        P("tok", "mem"),
        P("tok", "mem"),
        P("mem", "tok", None, None),
        P("tok", "mem", None),
        P("mem"),
        P("tok", "mem"),
    )
    out_specs = (P("tok", "mem"), P("tok", "mem"), P("tok", "mem"), P("tok", "mem"))
    return jax.shard_map(
        per_device, mesh=mesh, in_specs=in_specs, out_specs=out_specs, check_vma=False
    )
```

```python
import functools

import jax
import jax.numpy as jnp
from jax import lax
from jax.experimental import pallas as pl
from jax.experimental.pallas import tpu as pltpu
from jax.sharding import PartitionSpec as P

SPAN = 512
HALF = 256
BLOCK = 128
R = 4
HD = 128
NEG = -1e30
KIND = 512
VMEM_LIMIT = 56 * 2**20
BASE = 22
EXTRA = 10
ANY = pl.BlockSpec(memory_space=pl.ANY)
SMEM = pl.BlockSpec(memory_space=pltpu.SMEM)


def passed_along(block, axis, distance):
    devices = range(lax.axis_size(axis))
    route = [(i - distance, i) for i in devices if i - distance in devices]
    return lax.ppermute(block, axis, route)


def mm(a, b, dims):
    return lax.dot_general(a, b, (dims, ((), ())), preferred_element_type=jnp.float32)


def local_kernel(head, n_any, gates, prev_ok, q_ref, k_ref, v_ref, g_ref, halo_ref, *rest):
    (lo_ref, dq_ref, dk_ref, dv_ref, dkx_ref, dvx_ref, back_ref, token_ref,
     kx, vx, kt, vt, acc_k, acc_v) = rest[n_any:]
    scaling = HD ** -0.5
    keep = 1.0 - gates[head]
    kx[:SPAN] = halo_ref[:SPAN]
    kx[SPAN:] = k_ref[...]
    vx[:SPAN] = halo_ref[SPAN:]
    vx[SPAN:] = v_ref[...]
    kt[...] = kx[...].T
    vt[...] = vx[...].T
    ok = prev_ok[0] > 0
    tri = (lax.broadcasted_iota(jnp.int32, (HALF, HALF), 0)
           <= lax.broadcasted_iota(jnp.int32, (HALF, HALF), 1))
    for span in range(2):
        for half in range(2):
            row0 = span * SPAN + half * HALF
            win0 = span * SPAN
            width = SPAN + HALF * (half + 1)
            rows = pl.ds(row0, HALF)
            win = pl.ds(win0, width)
            q = q_ref[rows, :]
            gl = (keep * g_ref[rows, :].astype(jnp.float32)).astype(jnp.bfloat16)
            st = mm(kx[win, :], q, ((1,), (1,))) * scaling
            first = st[:SPAN]
            if span == 0:
                first = jnp.where(ok, first, NEG)
            parts = [first]
            if half:
                parts.append(st[SPAN:width - HALF])
            parts.append(jnp.where(tri, st[width - HALF:], NEG))
            st = jnp.concatenate(parts, axis=0)
            top = jnp.max(st, axis=0, keepdims=True)
            e = jnp.exp(st - top)
            total = jnp.sum(e, axis=0, keepdims=True)
            pt = (e * (1.0 / total)).astype(jnp.bfloat16)
            out_t = mm(vt[:, win], pt, ((1,), (0,)))
            gt = gl.astype(jnp.float32).T
            dot = jnp.sum(gt * out_t, axis=0, keepdims=True)
            dpt = mm(vx[win, :], gl, ((1,), (1,)))
            dst = (pt.astype(jnp.float32) * (dpt - dot)).astype(jnp.bfloat16)
            dq_t = mm(kt[:, win], dst, ((1,), (0,)))
            lo_ref[rows, :] = keep * out_t.T
            dq_ref[rows, :] = scaling * dq_t.T
            dkw = mm(dst, q, ((1,), (0,)))
            dvw = mm(pt, gl, ((1,), (0,)))
            if span == 0 and half == 0:
                acc_k[win, :] = dkw
                acc_v[win, :] = dvw
            else:
                old = 768 if span == 0 else (1024 if half == 0 else 1280)
                seen = max(0, min(old, win0 + width) - win0)
                acc_k[pl.ds(win0, seen), :] += dkw[:seen]
                acc_v[pl.ds(win0, seen), :] += dvw[:seen]
                if seen < width:
                    acc_k[pl.ds(win0 + seen, width - seen), :] = dkw[seen:]
                    acc_v[pl.ds(win0 + seen, width - seen), :] = dvw[seen:]
    back_ref[:SPAN] = (scaling * acc_k[:SPAN]).astype(jnp.bfloat16)
    back_ref[SPAN:] = acc_v[:SPAN].astype(jnp.bfloat16)
    dk_ref[...] = (scaling * acc_k[SPAN:2 * SPAN]).astype(jnp.bfloat16)
    dv_ref[...] = acc_v[SPAN:2 * SPAN].astype(jnp.bfloat16)
    dkx_ref[...] = scaling * acc_k[2 * SPAN:]
    dvx_ref[...] = acc_v[2 * SPAN:]
    token_ref[...] = jnp.zeros_like(token_ref)


def local_head(head, gates, prev_ok, q, k, v, g, halo, carry, after):
    rows, width = q.shape
    col = pl.BlockSpec((rows, HD), lambda i: (0, head))
    col_half = pl.BlockSpec((SPAN, HD), lambda i: (0, head))
    shapes = [
        jax.ShapeDtypeStruct((rows, width), jnp.float32),
        jax.ShapeDtypeStruct((rows, width), jnp.float32),
        jax.ShapeDtypeStruct((rows, width), jnp.bfloat16),
        jax.ShapeDtypeStruct((rows, width), jnp.bfloat16),
        jax.ShapeDtypeStruct((SPAN, width), jnp.float32),
        jax.ShapeDtypeStruct((SPAN, width), jnp.float32),
        jax.ShapeDtypeStruct((2 * SPAN, width), jnp.bfloat16),
        jax.ShapeDtypeStruct((8, 128), jnp.float32),
    ]
    extra = list(carry) + list(after)
    result = pl.pallas_call(
        functools.partial(local_kernel, head, len(extra)),
        grid=(1,),
        out_shape=shapes,
        in_specs=[SMEM, SMEM, col, col, col, col, col] + [ANY] * len(extra),
        out_specs=[col, col, col_half, col_half, col_half, col_half, col,
                   pl.BlockSpec((8, 128), lambda i: (0, 0))],
        scratch_shapes=[
            pltpu.VMEM((3 * SPAN, HD), jnp.bfloat16),
            pltpu.VMEM((3 * SPAN, HD), jnp.bfloat16),
            pltpu.VMEM((HD, 3 * SPAN), jnp.bfloat16),
            pltpu.VMEM((HD, 3 * SPAN), jnp.bfloat16),
            pltpu.VMEM((3 * SPAN, HD), jnp.float32),
            pltpu.VMEM((3 * SPAN, HD), jnp.float32),
        ],
        input_output_aliases={7 + i: i for i in range(len(carry))},
        compiler_params=pltpu.CompilerParams(vmem_limit_bytes=VMEM_LIMIT),
        cost_estimate=pl.CostEstimate(flops=9 * 10**9, bytes_accessed=4 * 2**20,
                                      transcendentals=2 * 512 * 896),
        name="local_head",
    )(gates, prev_ok, q, k, v, g, halo, *extra)
    return result[:7], result[7]


def memory_kernel(n_src, loc, gates, q_ref, g_ref, lo_ref, dqf_ref, dkx_ref, dvx_ref, back_ref,
                  dk_in, dv_in, *rest):
    sources = rest[:n_src]
    out_ref, dq_ref, dk_ref, dv_ref, buf, sems = rest[n_src:]
    head = pl.program_id(0)
    heads = pl.num_programs(0)
    scaling = HD ** -0.5

    def fetch(h, slot):
        for j in range(2 * R):
            code = loc[j // R, h, j % R]
            kind, index = code // KIND, lax.rem(code, KIND)

            def pick(low, high):
                if high - low == 1:
                    pltpu.make_async_copy(
                        sources[low].at[index], buf.at[slot, j], sems.at[slot, j]
                    ).start()
                    return
                middle = (low + high) // 2

                @pl.when(kind < middle)
                def _():
                    pick(low, middle)

                @pl.when(kind >= middle)
                def _():
                    pick(middle, high)

            pick(0, n_src)

    slot = lax.rem(head, 2)

    @pl.when(head == 0)
    def _():
        fetch(0, 0)

    @pl.when(head + 1 < heads)
    def _():
        fetch(head + 1, 1 - slot)

    dk_ref[...] = (dkx_ref[...] + back_ref[:SPAN].astype(jnp.float32)).astype(jnp.bfloat16)
    dv_ref[...] = (dvx_ref[...] + back_ref[SPAN:].astype(jnp.float32)).astype(jnp.bfloat16)
    for j in range(2 * R):
        pltpu.make_async_copy(sources[0].at[0], buf.at[slot, j], sems.at[slot, j]).wait()
    gate = gates[head]
    for span in range(2):
        blocks = buf[slot, pl.ds(span * R, R)]
        mk = blocks[:, :, :HD].reshape(R * BLOCK, HD)
        mv = blocks[:, :, HD:].reshape(R * BLOCK, HD)
        for half in range(2):
            rows = pl.ds(span * SPAN + half * HALF, HALF)
            q = q_ref[rows, :]
            gm = (gate * g_ref[rows, :].astype(jnp.float32)).astype(jnp.bfloat16)
            s = mm(q, mk, ((1,), (1,))) * scaling
            top = jnp.max(s, axis=1, keepdims=True)
            e = jnp.exp(s - top)
            total = jnp.sum(e, axis=1, keepdims=True)
            p = (e * (1.0 / total)).astype(jnp.bfloat16)
            mo = mm(p, mv, ((1,), (0,)))
            dp = mm(gm, mv, ((1,), (1,)))
            dot = jnp.sum(gm.astype(jnp.float32) * mo, axis=1, keepdims=True)
            ds = (p.astype(jnp.float32) * (dp - dot)).astype(jnp.bfloat16)
            dqm = mm(ds, mk, ((1,), (0,)))
            out_ref[rows, :] = (gate * mo + lo_ref[rows, :]).astype(jnp.bfloat16)
            dq_ref[rows, :] = (scaling * dqm + dqf_ref[rows, :]).astype(jnp.bfloat16)


def memory_heads(loc, gates, q, g, carry, back, sources):
    lo, dqf, dk, dv, dkx, dvx = carry[:6]
    rows, width = q.shape
    heads = width // HD
    col = pl.BlockSpec((rows, HD), lambda h: (0, h))
    col_half = pl.BlockSpec((SPAN, HD), lambda h: (0, h))
    lower = pl.BlockSpec((SPAN, HD), lambda h: (1, h))
    full = jax.ShapeDtypeStruct((rows, width), jnp.bfloat16)
    return pl.pallas_call(
        functools.partial(memory_kernel, len(sources)),
        grid=(heads,),
        out_shape=[full] * 4,
        in_specs=[SMEM, SMEM, col, col, col, col, col_half, col_half, col]
        + [ANY] * (2 + len(sources)),
        out_specs=[col, col, lower, lower],
        scratch_shapes=[
            pltpu.VMEM((2, 2 * R, BLOCK, 2 * HD), jnp.bfloat16),
            pltpu.SemaphoreType.DMA((2, 2 * R)),
        ],
        input_output_aliases={9: 2, 10: 3},
        compiler_params=pltpu.CompilerParams(vmem_limit_bytes=VMEM_LIMIT),
        cost_estimate=pl.CostEstimate(flops=heads * 4 * 2 * 2 * 512 * 512 * 128,
                                      bytes_accessed=24 * 2**20,
                                      transcendentals=heads * 2 * 512 * 512),
        name="memory_heads",
    )(loc, gates, q, g, lo, dqf, dkx, dvx, back, dk, dv, *sources)


def exchange_all(memory, block_ids):
    tok_count = lax.axis_size("tok")
    heads_here, blocks_here = memory.shape[:2]
    wanted = block_ids.reshape(-1)
    request_count = wanted.shape[0]
    owner_rank = wanted // blocks_here
    head_index = jnp.arange(request_count) // R % heads_here
    request_code = head_index * blocks_here + wanted % blocks_here
    order_ids = jnp.arange(request_count)
    same_owner = owner_rank[:, None] == owner_rank[None, :]
    slot_index = jnp.sum(same_owner & (order_ids[None, :] < order_ids[:, None]), axis=1)
    capacity = 2 * request_count // tok_count
    to_owner = (owner_rank[:, None] == jnp.arange(tok_count)[None, :]).astype(jnp.int32)
    to_slot = (slot_index[:, None] == jnp.arange(capacity)[None, :]).astype(jnp.int32)
    request_table = jnp.sum(
        request_code[:, None, None] * to_owner[:, :, None] * to_slot[:, None, :], axis=0
    )
    mem_flat = memory.reshape(-1, BLOCK, memory.shape[-1])
    found = mem_flat[lax.all_to_all(request_table, "tok", split_axis=0, concat_axis=0, tiled=True)]
    returned = lax.all_to_all(found, "tok", split_axis=0, concat_axis=0, tiled=True)
    loc = (owner_rank * capacity + slot_index).reshape(block_ids.shape)
    return returned.reshape(-1, BLOCK, memory.shape[-1]), loc.astype(jnp.int32)


def pack_kernel(lists, n_any, table, near, *rest):
    outs = rest[n_any:n_any + len(lists)]
    held, sems, sent = rest[-3:]
    for phase in range(2):
        number = 0
        for place, (row, start, count) in enumerate(lists):
            for j in range(count):
                code = table[row, start + j]

                @pl.when(code >= 0)
                def _():
                    copy = pltpu.make_async_copy(near.at[code], held.at[number], sems.at[number])
                    copy.wait() if phase else copy.start()
                number += 1
            if phase:
                pltpu.make_async_copy(
                    held.at[pl.ds(number - count, count)], outs[place], sent.at[place]
                ).start()
    number = 0
    for place, (row, start, count) in enumerate(lists):
        pltpu.make_async_copy(
            held.at[pl.ds(number, count)], outs[place], sent.at[place]
        ).wait()
        number += count


def pack(table, near, lists, after):
    total = sum(count for row, start, count in lists)
    return pl.pallas_call(
        functools.partial(pack_kernel, lists, len(after)),
        out_shape=[jax.ShapeDtypeStruct((n,) + near.shape[1:], near.dtype) for _, _, n in lists],
        in_specs=[SMEM, ANY] + [ANY] * len(after),
        out_specs=[ANY] * len(lists),
        scratch_shapes=[
            pltpu.VMEM((total,) + near.shape[1:], near.dtype),
            pltpu.SemaphoreType.DMA((total,)),
            pltpu.SemaphoreType.DMA((len(lists),)),
        ],
        compiler_params=pltpu.CompilerParams(vmem_limit_bytes=VMEM_LIMIT),
        cost_estimate=pl.CostEstimate(flops=0, bytes_accessed=total * 2**17, transcendentals=0),
        name="pack",
    )(table, near, *after)


def tails(keys, values, after):
    width = keys.shape[1]
    block = pl.BlockSpec((SPAN, width), lambda i: (keys.shape[0] // SPAN - 1, 0))

    def kernel(k_ref, v_ref, after_ref, out_ref):
        out_ref[:SPAN] = k_ref[...]
        out_ref[SPAN:] = v_ref[...]

    return pl.pallas_call(
        kernel,
        grid=(1,),
        out_shape=jax.ShapeDtypeStruct((2 * SPAN, width), keys.dtype),
        in_specs=[block, block, ANY],
        out_specs=pl.BlockSpec((2 * SPAN, width), lambda i: (0, 0)),
        compiler_params=pltpu.CompilerParams(vmem_limit_bytes=VMEM_LIMIT),
        name="tails",
    )(keys, values, after)


def summed(parts, after):
    def kernel(*refs):
        total = refs[0][...]
        for ref in refs[1:len(parts)]:
            total = total + ref[...]
        refs[-1][...] = total

    x = parts[0]
    whole = pl.BlockSpec(memory_space=pltpu.VMEM)
    return pl.pallas_call(
        kernel,
        out_shape=jax.ShapeDtypeStruct(x.shape, x.dtype),
        in_specs=[whole] * len(parts) + [ANY] * len(after),
        out_specs=whole,
        compiler_params=pltpu.CompilerParams(vmem_limit_bytes=VMEM_LIMIT),
        name="summed",
    )(*parts, *after)


def plan(block_ids, everyone, heads, blocks_here):
    tok_count = lax.axis_size("tok")
    chips = tok_count // 2
    shard = heads * blocks_here
    here = lax.axis_index("tok")
    chip, core = here // 2, here % 2
    head_of = jnp.arange(heads, dtype=jnp.int32)[None, :, None]
    block = (everyone // blocks_here) * shard + head_of * blocks_here + everyone % blocks_here
    universe = jnp.arange(tok_count * shard, dtype=jnp.int32)
    each = jnp.any(block.reshape(tok_count, -1)[:, :, None] == universe, axis=1)
    need = each.reshape(chips, 2, -1).any(axis=1).reshape(chips, tok_count, shard)
    sibling = lax.dynamic_slice(each, (here ^ 1, here * shard), (1, shard))
    away = jnp.arange(chips)[:, None] != jnp.arange(tok_count)[None, :] // 2
    most = jnp.max(jnp.sum(need.astype(jnp.int32), axis=2) * away, axis=0)
    before = jnp.triu(jnp.ones((shard, shard), jnp.bfloat16), 1)

    def ranked(wanted):
        rank = jnp.dot(wanted.astype(jnp.bfloat16), before, preferred_element_type=jnp.float32)
        return jnp.where(wanted, rank.astype(jnp.int32), -1)

    rank = ranked(need)
    from_me = lax.dynamic_index_in_dim(rank, here, 1, keepdims=False)
    sent = jnp.concatenate(
        [ranked(sibling)]
        + [lax.dynamic_slice_in_dim(from_me, (chip + k) % chips, 1, 0) for k in range(1, chips)]
    )
    slot = jnp.arange(BASE + EXTRA, dtype=jnp.int32)
    hit = sent[:, None, :] == slot[None, :, None]
    table = jnp.sum(jnp.where(hit, jnp.arange(1, shard + 1, dtype=jnp.int32), 0), axis=2) - 1
    sender = jnp.arange(tok_count, dtype=jnp.int32)[:, None]
    got = lax.dynamic_index_in_dim(rank, chip, 0, keepdims=False)
    away_by = (chip - sender // 2) % chips
    kind = jnp.where(got < BASE, 2 * away_by + (sender + core) % 2, 2 * chips)
    place = kind * KIND + jnp.where(got < BASE, got, got - BASE)
    mine = ranked(lax.dynamic_slice(each, (here, (here ^ 1) * shard), (1, shard)))
    place = jnp.where(sender == here, jnp.arange(shard, dtype=jnp.int32), place)
    place = jnp.where(sender == here ^ 1, KIND + mine, place).reshape(-1)
    own = (block_ids // blocks_here) * shard + head_of * blocks_here + block_ids % blocks_here
    loc = jnp.sum(jnp.where(own.reshape(-1, 1) == universe, place, 0), axis=1)
    return table, loc.reshape(block_ids.shape), most


def chip_shift(block, distance, only=None):
    count = lax.axis_size("tok")
    route = [(i, (i + 2 * distance) % count) for i in range(count) if only in (None, i)]
    return lax.ppermute(block, "tok", route)


def core_swap(block):
    return lax.ppermute(block, "tok", [(i, i ^ 1) for i in range(lax.axis_size("tok"))])


def most_of_all(most):
    count = lax.axis_size("mem")
    step = 1
    while step < count:
        other = lax.ppermute(most, "mem", [(i, i ^ step) for i in range(count)])
        most = jnp.maximum(most, other)
        step *= 2
    return most[:, 0]


def per_device(queries, keys, values, memory, block_ids, gate_bias, grad_out):
    my_rank = lax.axis_index("tok")
    tok_count = lax.axis_size("tok")
    heads, blocks_here = memory.shape[:2]
    chips = tok_count // 2
    direct = chips == 4 and lax.axis_size("mem") == 4
    gates = jax.nn.sigmoid(gate_bias)
    prev_ok = (my_rank > 0).astype(jnp.int32).reshape(1)
    if direct:
        everyone = lax.all_to_all(
            jnp.broadcast_to(block_ids[None], (tok_count,) + block_ids.shape),
            "tok", split_axis=0, concat_axis=0, tiled=True,
        )
    tail = tails(keys, values, everyone if direct else block_ids)
    halo = passed_along(tail, "tok", 1)
    carry, token = (), ()
    if direct:
        near = memory.reshape(-1, BLOCK, memory.shape[-1])
        table, loc, most = plan(block_ids, everyone, heads, blocks_here)
        most = most_of_all(jnp.broadcast_to(most[:, None], (tok_count, 128)))
        hot = jnp.argmax(most).astype(jnp.int32)
        overflow = jnp.any((most > BASE) & (jnp.arange(tok_count) != hot))
        one, three, side = pack(
            table, near, [(1, 0, BASE), (3, 0, BASE), (0, 0, 16)], (tail,)
        )
        two, *more = pack(
            table, near, [(2, 0, BASE)] + [(k, BASE, EXTRA) for k in range(1, chips)], (side,)
        )
        own_one = chip_shift(one, 1)
        own_three = chip_shift(three, 3)
        own_two = chip_shift(two, 2)
        beside = core_swap(side)
        token = (two,)
    for head in range(heads):
        carry, token = local_head(
            head, gates, prev_ok, queries, keys, values, grad_out, halo, carry, token
        )
        token = (token,)
        if direct and head == 3:
            token = token + (beside,)

    def finish(where, sources, back):
        return tuple(memory_heads(where, gates, queries, grad_out, carry, back, sources))

    def full_exchange(back):
        returned, where = exchange_all(memory, block_ids)
        return finish(where, [returned], back)

    if not direct:
        return full_exchange(passed_along(carry[6], "tok", -1))

    def from_device(source):
        def send(more, one, two, three, halo_grads):
            late = [chip_shift(more[k - 1], k, source) for k in range(1, chips)]
            back = passed_along(halo_grads, "tok", -1)
            passed = [core_swap(block) for block in (one, two, three)]
            late = summed(late, (back, *passed))
            return late + core_swap(late), back, *passed
        return send

    late, back, pass_one, pass_two, pass_three = lax.switch(
        hot, [from_device(source) for source in range(tok_count)],
        more, own_one, own_two, own_three, carry[6],
    )
    sources = [near, beside, own_one, pass_one, own_two, pass_two, own_three, pass_three, late]
    return lax.cond(
        overflow, lambda: full_exchange(back), lambda: finish(loc, sources, back)
    )


def solution(mesh):
    in_specs = (
        P("tok", "mem"),
        P("tok", "mem"),
        P("tok", "mem"),
        P("mem", "tok", None, None),
        P("tok", "mem", None),
        P("mem"),
        P("tok", "mem"),
    )
    out_specs = (P("tok", "mem"), P("tok", "mem"), P("tok", "mem"), P("tok", "mem"))
    return jax.shard_map(
        per_device, mesh=mesh, in_specs=in_specs, out_specs=out_specs, check_vma=False
    )
```

```python
import functools

import jax
import jax.numpy as jnp
from jax import lax
from jax.experimental import pallas as pl
from jax.experimental.pallas import tpu as pltpu
from jax.sharding import PartitionSpec as P

SPAN = 512
HALF = 256
BLOCK = 128
R = 4
HD = 128
NEG = -1e30
LOG2E = 1.4426950408889634
KIND = 512
VMEM_LIMIT = 56 * 2**20
MAIN = 18
SECOND = 7
ANY = pl.BlockSpec(memory_space=pl.ANY)
SMEM = pl.BlockSpec(memory_space=pltpu.SMEM)


def passed_along(block, axis, distance):
    devices = range(lax.axis_size(axis))
    route = [(i - distance, i) for i in devices if i - distance in devices]
    return lax.ppermute(block, axis, route)


def mm(a, b, dims):
    return lax.dot_general(a, b, (dims, ((), ())), preferred_element_type=jnp.float32)


def local_kernel(head, n_any, gates, prev_ok, q_ref, k_ref, v_ref, g_ref, halo_ref, *rest):
    (lo_ref, dq_ref, dk_ref, dv_ref, dkx_ref, dvx_ref, back_ref, token_ref,
     kx, vx, kt, vt, acc_k, acc_v) = rest[n_any:]
    scaling = HD ** -0.5
    keep = 1.0 - gates[head]
    kx[:SPAN] = halo_ref[:SPAN]
    kx[SPAN:] = k_ref[...]
    vx[:SPAN] = halo_ref[SPAN:]
    vx[SPAN:] = v_ref[...]
    kt[...] = kx[...].T
    vt[...] = vx[...].T
    ok = prev_ok[0] > 0
    tri = (lax.broadcasted_iota(jnp.int32, (HALF, HALF), 0)
           <= lax.broadcasted_iota(jnp.int32, (HALF, HALF), 1))
    for span in range(2):
        for half in range(2):
            row0 = span * SPAN + half * HALF
            win0 = span * SPAN
            width = SPAN + HALF * (half + 1)
            rows = pl.ds(row0, HALF)
            win = pl.ds(win0, width)
            q = q_ref[rows, :]
            gl = (keep * g_ref[rows, :].astype(jnp.float32)).astype(jnp.bfloat16)
            st = mm(kx[win, :], q, ((1,), (1,))) * scaling
            first = st[:SPAN]
            if span == 0:
                first = jnp.where(ok, first, NEG)
            parts = [first]
            if half:
                parts.append(st[SPAN:width - HALF])
            parts.append(jnp.where(tri, st[width - HALF:], NEG))
            st = jnp.concatenate(parts, axis=0)
            top = jnp.max(st, axis=0, keepdims=True)
            e = jnp.exp(st - top)
            total = jnp.sum(e, axis=0, keepdims=True)
            pt = (e * (1.0 / total)).astype(jnp.bfloat16)
            out_t = mm(vt[:, win], pt, ((1,), (0,)))
            gt = gl.astype(jnp.float32).T
            dot = jnp.sum(gt * out_t, axis=0, keepdims=True)
            dpt = mm(vx[win, :], gl, ((1,), (1,)))
            dst = (pt.astype(jnp.float32) * (dpt - dot)).astype(jnp.bfloat16)
            dq_t = mm(kt[:, win], dst, ((1,), (0,)))
            lo_ref[rows, :] = keep * out_t.T
            dq_ref[rows, :] = scaling * dq_t.T
            dkw = mm(dst, q, ((1,), (0,)))
            dvw = mm(pt, gl, ((1,), (0,)))
            if span == 0 and half == 0:
                acc_k[win, :] = dkw
                acc_v[win, :] = dvw
            else:
                old = 768 if span == 0 else (1024 if half == 0 else 1280)
                seen = max(0, min(old, win0 + width) - win0)
                acc_k[pl.ds(win0, seen), :] += dkw[:seen]
                acc_v[pl.ds(win0, seen), :] += dvw[:seen]
                if seen < width:
                    acc_k[pl.ds(win0 + seen, width - seen), :] = dkw[seen:]
                    acc_v[pl.ds(win0 + seen, width - seen), :] = dvw[seen:]
    back_ref[:SPAN] = (scaling * acc_k[:SPAN]).astype(jnp.bfloat16)
    back_ref[SPAN:] = acc_v[:SPAN].astype(jnp.bfloat16)
    dk_ref[...] = (scaling * acc_k[SPAN:2 * SPAN]).astype(jnp.bfloat16)
    dv_ref[...] = acc_v[SPAN:2 * SPAN].astype(jnp.bfloat16)
    dkx_ref[...] = scaling * acc_k[2 * SPAN:]
    dvx_ref[...] = acc_v[2 * SPAN:]
    token_ref[...] = jnp.zeros_like(token_ref)


def local_head(head, gates, prev_ok, q, k, v, g, halo, carry, after):
    rows, width = q.shape
    col = pl.BlockSpec((rows, HD), lambda i: (0, head))
    col_half = pl.BlockSpec((SPAN, HD), lambda i: (0, head))
    shapes = [
        jax.ShapeDtypeStruct((rows, width), jnp.float32),
        jax.ShapeDtypeStruct((rows, width), jnp.float32),
        jax.ShapeDtypeStruct((rows, width), jnp.bfloat16),
        jax.ShapeDtypeStruct((rows, width), jnp.bfloat16),
        jax.ShapeDtypeStruct((SPAN, width), jnp.float32),
        jax.ShapeDtypeStruct((SPAN, width), jnp.float32),
        jax.ShapeDtypeStruct((2 * SPAN, width), jnp.bfloat16),
        jax.ShapeDtypeStruct((8, 128), jnp.float32),
    ]
    extra = list(carry) + list(after)
    result = pl.pallas_call(
        functools.partial(local_kernel, head, len(extra)),
        grid=(1,),
        out_shape=shapes,
        in_specs=[SMEM, SMEM, col, col, col, col, col] + [ANY] * len(extra),
        out_specs=[col, col, col_half, col_half, col_half, col_half, col,
                   pl.BlockSpec((8, 128), lambda i: (0, 0))],
        scratch_shapes=[
            pltpu.VMEM((3 * SPAN, HD), jnp.bfloat16),
            pltpu.VMEM((3 * SPAN, HD), jnp.bfloat16),
            pltpu.VMEM((HD, 3 * SPAN), jnp.bfloat16),
            pltpu.VMEM((HD, 3 * SPAN), jnp.bfloat16),
            pltpu.VMEM((3 * SPAN, HD), jnp.float32),
            pltpu.VMEM((3 * SPAN, HD), jnp.float32),
        ],
        input_output_aliases={7 + i: i for i in range(len(carry))},
        compiler_params=pltpu.CompilerParams(vmem_limit_bytes=VMEM_LIMIT),
        cost_estimate=pl.CostEstimate(flops=9 * 10**9, bytes_accessed=4 * 2**20,
                                      transcendentals=2 * 512 * 896),
        name="local_head",
    )(gates, prev_ok, q, k, v, g, halo, *extra)
    return result[:7], result[7]


def memory_kernel(n_src, n_any, bounds, loc, gates, q_ref, g_ref, lo_ref, dqf_ref, *rest):
    sources = rest[:n_src]
    out_ref, dq_ref, token_ref, buf, sems = rest[n_src + n_any:]
    token_ref[...] = jnp.zeros_like(token_ref)
    head = pl.program_id(0)
    start, stop = bounds[0], bounds[1]
    scaling = HD ** -0.5

    def fetch(h, slot):
        for j in range(2 * R):
            code = loc[j // R, h, j % R]
            kind, index = code // KIND, lax.rem(code, KIND)

            def pick(low, high):
                if high - low == 1:
                    pltpu.make_async_copy(
                        sources[low].at[index], buf.at[slot, j], sems.at[slot, j]
                    ).start()
                    return
                middle = (low + high) // 2

                @pl.when(kind < middle)
                def _():
                    pick(low, middle)

                @pl.when(kind >= middle)
                def _():
                    pick(middle, high)

            pick(0, n_src)

    @pl.when((head == 0) & (start < stop))
    def _():
        fetch(start, lax.rem(start, 2))

    @pl.when((head >= start) & (head < stop))
    def _():
        slot = lax.rem(head, 2)

        @pl.when(head + 1 < stop)
        def _():
            fetch(head + 1, 1 - slot)

        for j in range(2 * R):
            pltpu.make_async_copy(sources[0].at[0], buf.at[slot, j], sems.at[slot, j]).wait()
        gate = gates[head]
        for span in range(2):
            blocks = buf[slot, pl.ds(span * R, R)]
            mk = blocks[:, :, :HD].reshape(R * BLOCK, HD)
            mv = blocks[:, :, HD:].reshape(R * BLOCK, HD)
            rows = pl.ds(span * SPAN, SPAN)
            q = q_ref[rows, :]
            gm = (gate * g_ref[rows, :].astype(jnp.float32)).astype(jnp.bfloat16)
            s = mm(q, mk, ((1,), (1,)))
            top = jnp.max(s, axis=1, keepdims=True)
            e = jnp.exp2((s - top) * (scaling * LOG2E))
            share = 1.0 / jnp.sum(e, axis=1, keepdims=True)
            mo = mm(e.astype(jnp.bfloat16), mv, ((1,), (0,))) * share
            dp = mm(gm, mv, ((1,), (1,)))
            dot = jnp.sum(gm.astype(jnp.float32) * mo, axis=1, keepdims=True)
            ds = (e * (dp - dot)).astype(jnp.bfloat16)
            dqm = mm(ds, mk, ((1,), (0,))) * (share * scaling)
            out_ref[rows, :] = (gate * mo + lo_ref[rows, :]).astype(jnp.bfloat16)
            dq_ref[rows, :] = (dqm + dqf_ref[rows, :]).astype(jnp.bfloat16)


def memory_heads(start, stop, loc, gates, q, g, carry, sources, made, after=()):
    rows, width = q.shape
    heads = width // HD
    bounds = jnp.stack([jnp.int32(start), jnp.int32(stop)])

    def column(h, bounds):
        return 0, jnp.clip(h, bounds[0], jnp.maximum(bounds[1] - 1, bounds[0]))

    col = pl.BlockSpec((rows, HD), column)
    full = jax.ShapeDtypeStruct((rows, width), jnp.bfloat16)
    extra = list(made) + list(after)
    return pl.pallas_call(
        functools.partial(memory_kernel, len(sources), len(extra)),
        grid_spec=pltpu.PrefetchScalarGridSpec(
            num_scalar_prefetch=1,
            grid=(heads,),
            in_specs=[SMEM, SMEM, col, col, col, col] + [ANY] * (len(sources) + len(extra)),
            out_specs=[col, col, pl.BlockSpec((16, 128), lambda h, bounds: (0, 0))],
            scratch_shapes=[
                pltpu.VMEM((2, 2 * R, BLOCK, 2 * HD), jnp.bfloat16),
                pltpu.SemaphoreType.DMA((2, 2 * R)),
            ],
        ),
        out_shape=[full, full, jax.ShapeDtypeStruct((16, 128), jnp.bfloat16)],
        input_output_aliases={7 + len(sources) + i: i for i in range(len(made))},
        compiler_params=pltpu.CompilerParams(vmem_limit_bytes=VMEM_LIMIT),
        cost_estimate=pl.CostEstimate(flops=14 * 10**9, bytes_accessed=2**20,
                                      transcendentals=heads * 2 * 512 * 512),
        name="memory_heads",
    )(bounds, loc, gates, q, g, carry[0], carry[1], *sources, *extra)


def close_kernel(dkx_ref, dvx_ref, back_ref, dk_in, dv_in, after_ref, dk_ref, dv_ref):
    dk_ref[...] = (dkx_ref[...] + back_ref[:SPAN].astype(jnp.float32)).astype(jnp.bfloat16)
    dv_ref[...] = (dvx_ref[...] + back_ref[SPAN:].astype(jnp.float32)).astype(jnp.bfloat16)


def close_grads(carry, back, after):
    dk, dv, dkx, dvx = carry[2:6]
    width = dk.shape[1]
    part = width // 4
    upper = pl.BlockSpec((SPAN, part), lambda h: (0, h))
    lower = pl.BlockSpec((SPAN, part), lambda h: (1, h))
    return pl.pallas_call(
        close_kernel,
        grid=(4,),
        out_shape=[jax.ShapeDtypeStruct(dk.shape, dk.dtype)] * 2,
        in_specs=[upper, upper, pl.BlockSpec((2 * SPAN, part), lambda h: (0, h))] + [ANY] * 3,
        out_specs=[lower, lower],
        input_output_aliases={3: 0, 4: 1},
        compiler_params=pltpu.CompilerParams(vmem_limit_bytes=VMEM_LIMIT),
        name="close_grads",
    )(dkx, dvx, back, dk, dv, after)


def exchange_all(memory, block_ids):
    tok_count = lax.axis_size("tok")
    heads_here, blocks_here = memory.shape[:2]
    wanted = block_ids.reshape(-1)
    request_count = wanted.shape[0]
    owner_rank = wanted // blocks_here
    head_index = jnp.arange(request_count) // R % heads_here
    request_code = head_index * blocks_here + wanted % blocks_here
    order_ids = jnp.arange(request_count)
    same_owner = owner_rank[:, None] == owner_rank[None, :]
    slot_index = jnp.sum(same_owner & (order_ids[None, :] < order_ids[:, None]), axis=1)
    capacity = 2 * request_count // tok_count
    to_owner = (owner_rank[:, None] == jnp.arange(tok_count)[None, :]).astype(jnp.int32)
    to_slot = (slot_index[:, None] == jnp.arange(capacity)[None, :]).astype(jnp.int32)
    request_table = jnp.sum(
        request_code[:, None, None] * to_owner[:, :, None] * to_slot[:, None, :], axis=0
    )
    mem_flat = memory.reshape(-1, BLOCK, memory.shape[-1])
    found = mem_flat[lax.all_to_all(request_table, "tok", split_axis=0, concat_axis=0, tiled=True)]
    returned = lax.all_to_all(found, "tok", split_axis=0, concat_axis=0, tiled=True)
    loc = (owner_rank * capacity + slot_index).reshape(block_ids.shape)
    return returned.reshape(-1, BLOCK, memory.shape[-1]), loc.astype(jnp.int32)


def pack_kernel(groups, n_src, n_any, table, *rest):
    sources = rest[:n_src]
    outs = rest[n_src + n_any:n_src + n_any + len(groups)]
    held, sems, sent = rest[-3:]
    sizes = [sum(count for row, count in group) for group in groups]
    for phase in range(2):
        number = 0
        for place, group in enumerate(groups):
            for row, count in group:
                for j in range(count):
                    code = table[row, j]
                    for kind, source in enumerate(sources):
                        @pl.when((code >= kind * KIND) & (code < (kind + 1) * KIND))
                        def _():
                            copy = pltpu.make_async_copy(
                                source.at[code - kind * KIND], held.at[number], sems.at[number]
                            )
                            copy.wait() if phase else copy.start()
                    number += 1
            if phase:
                pltpu.make_async_copy(
                    held.at[pl.ds(number - sizes[place], sizes[place])], outs[place],
                    sent.at[place],
                ).start()
    number = 0
    for place, size in enumerate(sizes):
        pltpu.make_async_copy(held.at[pl.ds(number, size)], outs[place], sent.at[place]).wait()
        number += size


def pack(table, sources, groups, after):
    sizes = [sum(count for row, count in group) for group in groups]
    block = sources[0].shape[1:]
    kind = sources[0].dtype
    return pl.pallas_call(
        functools.partial(pack_kernel, groups, len(sources), len(after)),
        out_shape=[jax.ShapeDtypeStruct((size,) + block, kind) for size in sizes],
        in_specs=[SMEM] + [ANY] * (len(sources) + len(after)),
        out_specs=[ANY] * len(groups),
        scratch_shapes=[
            pltpu.VMEM((sum(sizes),) + block, kind),
            pltpu.SemaphoreType.DMA((sum(sizes),)),
            pltpu.SemaphoreType.DMA((len(groups),)),
        ],
        compiler_params=pltpu.CompilerParams(vmem_limit_bytes=VMEM_LIMIT),
        cost_estimate=pl.CostEstimate(flops=0, bytes_accessed=2**16, transcendentals=0),
        name="pack",
    )(table, *sources, *after)


def held_back(x, after):
    def kernel(*refs):
        pass

    return pl.pallas_call(
        kernel,
        out_shape=jax.ShapeDtypeStruct(x.shape, x.dtype),
        in_specs=[ANY] * (1 + len(after)),
        out_specs=ANY,
        input_output_aliases={0: 0},
        cost_estimate=pl.CostEstimate(flops=0, bytes_accessed=0, transcendentals=0),
        name="held_back",
    )(x, *after)


def tails(keys, values, after):
    width = keys.shape[1]
    block = pl.BlockSpec((SPAN, width), lambda i: (keys.shape[0] // SPAN - 1, 0))

    def kernel(k_ref, v_ref, after_ref, out_ref):
        out_ref[:SPAN] = k_ref[...]
        out_ref[SPAN:] = v_ref[...]

    return pl.pallas_call(
        kernel,
        grid=(1,),
        out_shape=jax.ShapeDtypeStruct((2 * SPAN, width), keys.dtype),
        in_specs=[block, block, ANY],
        out_specs=pl.BlockSpec((2 * SPAN, width), lambda i: (0, 0)),
        compiler_params=pltpu.CompilerParams(vmem_limit_bytes=VMEM_LIMIT),
        name="tails",
    )(keys, values, after)


def plan(block_ids, everyone, heads, blocks_here):
    tok_count = lax.axis_size("tok")
    chips = tok_count // 2
    shard = heads * blocks_here
    here = lax.axis_index("tok")
    chip, core = here // 2, here % 2
    head_of = jnp.arange(heads, dtype=jnp.int32)[None, :, None]
    block = (everyone // blocks_here) * shard + head_of * blocks_here + everyone % blocks_here
    universe = jnp.arange(tok_count * shard, dtype=jnp.int32)
    each = jnp.any(block.reshape(tok_count, -1)[:, :, None] == universe, axis=1)
    need = each.reshape(chips, 2, -1).any(axis=1).reshape(chips, tok_count, shard)
    sibling = lax.dynamic_slice(each, (here ^ 1, here * shard), (1, shard))
    before = jnp.triu(jnp.ones((shard, shard), jnp.bfloat16), 1)

    def ranked(wanted):
        rank = jnp.dot(wanted.astype(jnp.bfloat16), before, preferred_element_type=jnp.float32)
        return jnp.where(wanted, rank.astype(jnp.int32), -1)

    rank = ranked(need)
    left = jnp.maximum(jnp.sum(need.astype(jnp.int32), axis=2) - MAIN, 0)
    pairs = left.reshape(chips, chips, 2)
    most = jnp.max(jnp.where(jnp.eye(chips, dtype=bool), 0, pairs.sum(axis=2)))
    ahead = jnp.stack([jnp.zeros_like(pairs[..., 0]), pairs[..., 0]], axis=2).reshape(left.shape)
    pooled = jnp.where(rank >= MAIN, rank - MAIN + ahead[:, :, None], -1)

    chip_ids = jnp.arange(chips, dtype=jnp.int32)[:, None]

    def to_others(ranks, device, at_home=-1):
        mine = lax.dynamic_index_in_dim(ranks, device, 1, keepdims=False)
        return jnp.where(chip_ids == chip, at_home, mine)

    slot = jnp.arange(MAIN, dtype=jnp.int32)
    index = jnp.arange(1, shard + 1, dtype=jnp.int32)

    def listed(ranks, slots):
        hit = ranks[:, None, :] == slots[None, :, None]
        return jnp.sum(jnp.where(hit, index, 0), axis=2) - 1

    handed = to_others(pooled, here ^ 1)[:, None, :] == 2 * slot[None, :, None] + core
    from_side = KIND + SECOND * chip_ids + slot
    own_left = to_others(pooled, here)
    second = listed(own_left, 2 * slot + core)
    table = jnp.concatenate([
        listed(to_others(rank, here, ranked(sibling)), slot),
        listed(own_left, 2 * slot + 1 - core),
        jnp.where(jnp.any(handed, axis=2), from_side, second),
    ])
    sender = jnp.arange(tok_count, dtype=jnp.int32)[:, None]
    got = lax.dynamic_index_in_dim(rank, chip, 0, keepdims=False)
    rest = lax.dynamic_index_in_dim(pooled, chip, 0, keepdims=False)
    main_place = (1 + (sender + core) % 2) * KIND + MAIN * (sender // 2) + got
    rest_place = (3 + (rest + core) % 2) * KIND + SECOND * (sender // 2) + rest // 2
    place = jnp.where(got < MAIN, main_place, rest_place)
    mine = ranked(lax.dynamic_slice(each, (here, (here ^ 1) * shard), (1, shard)))
    place = jnp.where(sender == here, jnp.arange(shard, dtype=jnp.int32), place)
    place = jnp.where(sender == here ^ 1, 2 * KIND + MAIN * chip + mine, place).reshape(-1)
    own = (block_ids // blocks_here) * shard + head_of * blocks_here + block_ids % blocks_here
    loc = jnp.sum(jnp.where(own.reshape(-1, 1) == universe, place, 0), axis=1)
    loc = loc.reshape(block_ids.shape)
    waits = jnp.any(loc >= 3 * KIND, axis=(0, 2))
    ready = jnp.min(jnp.where(waits, jnp.arange(heads), heads - 1))
    return table, loc, most, ready


def between_chips(block):
    count = lax.axis_size("tok")
    groups = [[i for i in range(count) if i % 2 == core] for core in range(2)]
    return lax.all_to_all(
        block, "tok", split_axis=0, concat_axis=0, axis_index_groups=groups, tiled=True
    )


def core_swap(block):
    return lax.ppermute(block, "tok", [(i, i ^ 1) for i in range(lax.axis_size("tok"))])


def most_of_all(most):
    count = lax.axis_size("mem")
    step = 1
    while step < count:
        other = lax.ppermute(most, "mem", [(i, i ^ step) for i in range(count)])
        most = jnp.maximum(most, other)
        step *= 2
    return most


def per_device(queries, keys, values, memory, block_ids, gate_bias, grad_out):
    my_rank = lax.axis_index("tok")
    tok_count = lax.axis_size("tok")
    heads, blocks_here = memory.shape[:2]
    chips = tok_count // 2
    direct = chips == 4 and lax.axis_size("mem") == 4
    gates = jax.nn.sigmoid(gate_bias)
    prev_ok = (my_rank > 0).astype(jnp.int32).reshape(1)
    if direct:
        everyone = lax.all_to_all(
            jnp.broadcast_to(block_ids[None], (tok_count,) + block_ids.shape),
            "tok", split_axis=0, concat_axis=0, tiled=True,
        )
    tail = tails(keys, values, block_ids)
    halo = passed_along(tail, "tok", 1)
    carry, token = (), ()
    if direct:
        near = memory.reshape(-1, BLOCK, memory.shape[-1])
        table, loc, most, ready = plan(block_ids, everyone, heads, blocks_here)
        (main,) = pack(table, [near], [[(chip, MAIN) for chip in range(chips)]], (tail,))
        own_main = between_chips(main)
        (side,) = pack(
            table, [near], [[(chips + chip, SECOND) for chip in range(chips)]], (main,)
        )
        handed = core_swap(side)
        token = (side,)
    for head in range(heads):
        if direct and head == 4:
            token = token + (loc, most)
        carry, token = local_head(
            head, gates, prev_ok, queries, keys, values, grad_out, halo, carry, token
        )
        if direct and head == 1:
            most = most_of_all(jnp.broadcast_to(most, (8, 128)) + token.astype(jnp.int32))
            overflow = most[0, 0] > 2 * SECOND
        token = (token,)
    back = passed_along(carry[6], "tok", -1)

    def finish(start, where, sources, made, after=()):
        return tuple(memory_heads(
            start, heads, where, gates, queries, grad_out, carry, sources, made, after
        )[:2])

    def full_exchange():
        returned, where = exchange_all(memory, block_ids)
        return finish(0, where, [returned], ())

    if not direct:
        return full_exchange() + tuple(close_grads(carry, back, block_ids))
    (second,) = pack(
        table, [near, handed],
        [[(2 * chips + chip, SECOND) for chip in range(chips)]], token,
    )
    own_second = between_chips(second)
    own_main = held_back(own_main, (second,))
    sources = [near, own_main, core_swap(own_main)]
    *made, made_token = memory_heads(
        0, jnp.where(overflow, 0, ready), loc, gates, queries, grad_out, carry, sources, ()
    )
    own_second = held_back(own_second, (made_token,))
    sources += [own_second, core_swap(own_second)]
    out, dq = lax.cond(
        overflow, full_exchange, lambda: finish(ready, loc, sources, made)
    )
    dk, dv = close_grads(carry, back, out)
    return out, dq, dk, dv


def solution(mesh):
    in_specs = (
        P("tok", "mem"),
        P("tok", "mem"),
        P("tok", "mem"),
        P("mem", "tok", None, None),
        P("tok", "mem", None),
        P("mem"),
        P("tok", "mem"),
    )
    out_specs = (P("tok", "mem"), P("tok", "mem"), P("tok", "mem"), P("tok", "mem"))
    return jax.shard_map(
        per_device, mesh=mesh, in_specs=in_specs, out_specs=out_specs, check_vma=False
    )
```

```python
import functools

import jax
import jax.numpy as jnp
from jax import lax
from jax.experimental import pallas as pl
from jax.experimental.pallas import tpu as pltpu
from jax.sharding import PartitionSpec as P

SPAN = 512
HALF = 256
BLOCK = 128
R = 4
HD = 128
NEG = -1e30
LOG2E = 1.4426950408889634
KIND = 512
VMEM_LIMIT = 56 * 2**20
MAIN = 19
HANDED = 8
SECOND = 6
ANY = pl.BlockSpec(memory_space=pl.ANY)
SMEM = pl.BlockSpec(memory_space=pltpu.SMEM)


def passed_along(block, axis, distance):
    devices = range(lax.axis_size(axis))
    route = [(i - distance, i) for i in devices if i - distance in devices]
    return lax.ppermute(block, axis, route)


def mm(a, b, dims):
    return lax.dot_general(a, b, (dims, ((), ())), preferred_element_type=jnp.float32)


def local_kernel(head, n_any, gates, prev_ok, q_ref, k_ref, v_ref, g_ref, halo_ref, *rest):
    (lo_ref, dq_ref, dk_ref, dv_ref, dkx_ref, dvx_ref, back_ref, token_ref,
     kx, vx, kt, vt, acc_k, acc_v) = rest[n_any:]
    scaling = HD ** -0.5
    keep = 1.0 - gates[head]
    kx[:SPAN] = halo_ref[:SPAN]
    kx[SPAN:] = k_ref[...]
    vx[:SPAN] = halo_ref[SPAN:]
    vx[SPAN:] = v_ref[...]
    kt[...] = kx[...].T
    vt[...] = vx[...].T
    ok = prev_ok[0] > 0
    tri = (lax.broadcasted_iota(jnp.int32, (HALF, HALF), 0)
           <= lax.broadcasted_iota(jnp.int32, (HALF, HALF), 1))
    for span in range(2):
        for half in range(2):
            row0 = span * SPAN + half * HALF
            win0 = span * SPAN
            width = SPAN + HALF * (half + 1)
            rows = pl.ds(row0, HALF)
            win = pl.ds(win0, width)
            q = q_ref[rows, :]
            gl = (keep * g_ref[rows, :].astype(jnp.float32)).astype(jnp.bfloat16)
            st = mm(kx[win, :], q, ((1,), (1,))) * scaling
            first = st[:SPAN]
            if span == 0:
                first = jnp.where(ok, first, NEG)
            parts = [first]
            if half:
                parts.append(st[SPAN:width - HALF])
            parts.append(jnp.where(tri, st[width - HALF:], NEG))
            st = jnp.concatenate(parts, axis=0)
            top = jnp.max(st, axis=0, keepdims=True)
            e = jnp.exp(st - top)
            total = jnp.sum(e, axis=0, keepdims=True)
            pt = (e * (1.0 / total)).astype(jnp.bfloat16)
            out_t = mm(vt[:, win], pt, ((1,), (0,)))
            gt = gl.astype(jnp.float32).T
            dot = jnp.sum(gt * out_t, axis=0, keepdims=True)
            dpt = mm(vx[win, :], gl, ((1,), (1,)))
            dst = (pt.astype(jnp.float32) * (dpt - dot)).astype(jnp.bfloat16)
            dq_t = mm(kt[:, win], dst, ((1,), (0,)))
            lo_ref[rows, :] = keep * out_t.T
            dq_ref[rows, :] = scaling * dq_t.T
            dkw = mm(dst, q, ((1,), (0,)))
            dvw = mm(pt, gl, ((1,), (0,)))
            if span == 0 and half == 0:
                acc_k[win, :] = dkw
                acc_v[win, :] = dvw
            else:
                old = 768 if span == 0 else (1024 if half == 0 else 1280)
                seen = max(0, min(old, win0 + width) - win0)
                acc_k[pl.ds(win0, seen), :] += dkw[:seen]
                acc_v[pl.ds(win0, seen), :] += dvw[:seen]
                if seen < width:
                    acc_k[pl.ds(win0 + seen, width - seen), :] = dkw[seen:]
                    acc_v[pl.ds(win0 + seen, width - seen), :] = dvw[seen:]
    back_ref[:SPAN] = (scaling * acc_k[:SPAN]).astype(jnp.bfloat16)
    back_ref[SPAN:] = acc_v[:SPAN].astype(jnp.bfloat16)
    dk_ref[...] = (scaling * acc_k[SPAN:2 * SPAN]).astype(jnp.bfloat16)
    dv_ref[...] = acc_v[SPAN:2 * SPAN].astype(jnp.bfloat16)
    dkx_ref[...] = scaling * acc_k[2 * SPAN:]
    dvx_ref[...] = acc_v[2 * SPAN:]
    token_ref[...] = jnp.zeros_like(token_ref)


def local_head(head, gates, prev_ok, q, k, v, g, halo, carry, after):
    rows, width = q.shape
    col = pl.BlockSpec((rows, HD), lambda i: (0, head))
    col_half = pl.BlockSpec((SPAN, HD), lambda i: (0, head))
    shapes = [
        jax.ShapeDtypeStruct((rows, width), jnp.float32),
        jax.ShapeDtypeStruct((rows, width), jnp.float32),
        jax.ShapeDtypeStruct((rows, width), jnp.bfloat16),
        jax.ShapeDtypeStruct((rows, width), jnp.bfloat16),
        jax.ShapeDtypeStruct((SPAN, width), jnp.float32),
        jax.ShapeDtypeStruct((SPAN, width), jnp.float32),
        jax.ShapeDtypeStruct((2 * SPAN, width), jnp.bfloat16),
        jax.ShapeDtypeStruct((8, 128), jnp.float32),
    ]
    extra = list(carry) + list(after)
    result = pl.pallas_call(
        functools.partial(local_kernel, head, len(extra)),
        grid=(1,),
        out_shape=shapes,
        in_specs=[SMEM, SMEM, col, col, col, col, col] + [ANY] * len(extra),
        out_specs=[col, col, col_half, col_half, col_half, col_half, col,
                   pl.BlockSpec((8, 128), lambda i: (0, 0))],
        scratch_shapes=[
            pltpu.VMEM((3 * SPAN, HD), jnp.bfloat16),
            pltpu.VMEM((3 * SPAN, HD), jnp.bfloat16),
            pltpu.VMEM((HD, 3 * SPAN), jnp.bfloat16),
            pltpu.VMEM((HD, 3 * SPAN), jnp.bfloat16),
            pltpu.VMEM((3 * SPAN, HD), jnp.float32),
            pltpu.VMEM((3 * SPAN, HD), jnp.float32),
        ],
        input_output_aliases={7 + i: i for i in range(len(carry))},
        compiler_params=pltpu.CompilerParams(vmem_limit_bytes=VMEM_LIMIT),
        cost_estimate=pl.CostEstimate(flops=9 * 10**9, bytes_accessed=4 * 2**20,
                                      transcendentals=2 * 512 * 896),
        name="local_head",
    )(gates, prev_ok, q, k, v, g, halo, *extra)
    return result[:7], result[7]


def memory_kernel(n_src, n_any, bounds, loc, gates, q_ref, g_ref, lo_ref, dqf_ref, *rest):
    sources = rest[:n_src]
    out_ref, dq_ref, token_ref, buf, sems = rest[n_src + n_any:]
    token_ref[...] = jnp.zeros_like(token_ref)
    head = pl.program_id(0)
    start, stop = bounds[0], bounds[1]
    scaling = HD ** -0.5

    def fetch(h, slot):
        for j in range(2 * R):
            code = loc[j // R, h, j % R]
            kind, index = code // KIND, lax.rem(code, KIND)

            def pick(low, high):
                if high - low == 1:
                    pltpu.make_async_copy(
                        sources[low].at[index], buf.at[slot, j], sems.at[slot, j]
                    ).start()
                    return
                middle = (low + high) // 2

                @pl.when(kind < middle)
                def _():
                    pick(low, middle)

                @pl.when(kind >= middle)
                def _():
                    pick(middle, high)

            pick(0, n_src)

    @pl.when((head == 0) & (start < stop))
    def _():
        fetch(start, lax.rem(start, 2))

    @pl.when((head >= start) & (head < stop))
    def _():
        slot = lax.rem(head, 2)

        @pl.when(head + 1 < stop)
        def _():
            fetch(head + 1, 1 - slot)

        for j in range(2 * R):
            pltpu.make_async_copy(sources[0].at[0], buf.at[slot, j], sems.at[slot, j]).wait()
        gate = gates[head]
        for span in range(2):
            blocks = buf[slot, pl.ds(span * R, R)]
            mk = blocks[:, :, :HD].reshape(R * BLOCK, HD)
            mv = blocks[:, :, HD:].reshape(R * BLOCK, HD)
            rows = pl.ds(span * SPAN, SPAN)
            q = q_ref[rows, :]
            gm = (gate * g_ref[rows, :].astype(jnp.float32)).astype(jnp.bfloat16)
            s = mm(q, mk, ((1,), (1,)))
            top = jnp.max(s, axis=1, keepdims=True)
            e = jnp.exp2((s - top) * (scaling * LOG2E))
            share = 1.0 / jnp.sum(e, axis=1, keepdims=True)
            mo = mm(e.astype(jnp.bfloat16), mv, ((1,), (0,))) * share
            dp = mm(gm, mv, ((1,), (1,)))
            dot = jnp.sum(gm.astype(jnp.float32) * mo, axis=1, keepdims=True)
            ds = (e * (dp - dot)).astype(jnp.bfloat16)
            dqm = mm(ds, mk, ((1,), (0,))) * (share * scaling)
            out_ref[rows, :] = (gate * mo + lo_ref[rows, :]).astype(jnp.bfloat16)
            dq_ref[rows, :] = (dqm + dqf_ref[rows, :]).astype(jnp.bfloat16)


def memory_heads(start, stop, loc, gates, q, g, carry, sources, made, after=()):
    rows, width = q.shape
    heads = width // HD
    bounds = jnp.stack([jnp.int32(start), jnp.int32(stop)])

    def column(h, bounds):
        return 0, jnp.clip(h, bounds[0], jnp.maximum(bounds[1] - 1, bounds[0]))

    col = pl.BlockSpec((rows, HD), column)
    full = jax.ShapeDtypeStruct((rows, width), jnp.bfloat16)
    extra = list(made) + list(after)
    return pl.pallas_call(
        functools.partial(memory_kernel, len(sources), len(extra)),
        grid_spec=pltpu.PrefetchScalarGridSpec(
            num_scalar_prefetch=1,
            grid=(heads,),
            in_specs=[SMEM, SMEM, col, col, col, col] + [ANY] * (len(sources) + len(extra)),
            out_specs=[col, col, pl.BlockSpec((16, 128), lambda h, bounds: (0, 0))],
            scratch_shapes=[
                pltpu.VMEM((2, 2 * R, BLOCK, 2 * HD), jnp.bfloat16),
                pltpu.SemaphoreType.DMA((2, 2 * R)),
            ],
        ),
        out_shape=[full, full, jax.ShapeDtypeStruct((16, 128), jnp.bfloat16)],
        input_output_aliases={7 + len(sources) + i: i for i in range(len(made))},
        compiler_params=pltpu.CompilerParams(vmem_limit_bytes=VMEM_LIMIT),
        cost_estimate=pl.CostEstimate(flops=14 * 10**9, bytes_accessed=2**20,
                                      transcendentals=heads * 2 * 512 * 512),
        name="memory_heads",
    )(bounds, loc, gates, q, g, carry[0], carry[1], *sources, *extra)


def close_kernel(dkx_ref, dvx_ref, back_ref, dk_in, dv_in, after_ref, dk_ref, dv_ref):
    dk_ref[...] = (dkx_ref[...] + back_ref[:SPAN].astype(jnp.float32)).astype(jnp.bfloat16)
    dv_ref[...] = (dvx_ref[...] + back_ref[SPAN:].astype(jnp.float32)).astype(jnp.bfloat16)


def close_grads(carry, back, after):
    dk, dv, dkx, dvx = carry[2:6]
    width = dk.shape[1]
    part = width // 4
    upper = pl.BlockSpec((SPAN, part), lambda h: (0, h))
    lower = pl.BlockSpec((SPAN, part), lambda h: (1, h))
    return pl.pallas_call(
        close_kernel,
        grid=(4,),
        out_shape=[jax.ShapeDtypeStruct(dk.shape, dk.dtype)] * 2,
        in_specs=[upper, upper, pl.BlockSpec((2 * SPAN, part), lambda h: (0, h))] + [ANY] * 3,
        out_specs=[lower, lower],
        input_output_aliases={3: 0, 4: 1},
        compiler_params=pltpu.CompilerParams(vmem_limit_bytes=VMEM_LIMIT),
        name="close_grads",
    )(dkx, dvx, back, dk, dv, after)


def exchange_all(memory, block_ids):
    tok_count = lax.axis_size("tok")
    heads_here, blocks_here = memory.shape[:2]
    wanted = block_ids.reshape(-1)
    request_count = wanted.shape[0]
    owner_rank = wanted // blocks_here
    head_index = jnp.arange(request_count) // R % heads_here
    request_code = head_index * blocks_here + wanted % blocks_here
    order_ids = jnp.arange(request_count)
    same_owner = owner_rank[:, None] == owner_rank[None, :]
    slot_index = jnp.sum(same_owner & (order_ids[None, :] < order_ids[:, None]), axis=1)
    capacity = 2 * request_count // tok_count
    to_owner = (owner_rank[:, None] == jnp.arange(tok_count)[None, :]).astype(jnp.int32)
    to_slot = (slot_index[:, None] == jnp.arange(capacity)[None, :]).astype(jnp.int32)
    request_table = jnp.sum(
        request_code[:, None, None] * to_owner[:, :, None] * to_slot[:, None, :], axis=0
    )
    mem_flat = memory.reshape(-1, BLOCK, memory.shape[-1])
    found = mem_flat[lax.all_to_all(request_table, "tok", split_axis=0, concat_axis=0, tiled=True)]
    returned = lax.all_to_all(found, "tok", split_axis=0, concat_axis=0, tiled=True)
    loc = (owner_rank * capacity + slot_index).reshape(block_ids.shape)
    return returned.reshape(-1, BLOCK, memory.shape[-1]), loc.astype(jnp.int32)


def pack_kernel(groups, n_src, n_any, table, *rest):
    sources = rest[:n_src]
    outs = rest[n_src + n_any:n_src + n_any + len(groups)]
    held, sems, sent = rest[-3:]
    sizes = [sum(count for row, count in group) for group in groups]
    for phase in range(2):
        number = 0
        for place, group in enumerate(groups):
            for row, count in group:
                for j in range(count):
                    code = table[row, j]
                    for kind, source in enumerate(sources):
                        @pl.when((code >= kind * KIND) & (code < (kind + 1) * KIND))
                        def _():
                            copy = pltpu.make_async_copy(
                                source.at[code - kind * KIND], held.at[number], sems.at[number]
                            )
                            copy.wait() if phase else copy.start()
                    number += 1
            if phase:
                pltpu.make_async_copy(
                    held.at[pl.ds(number - sizes[place], sizes[place])], outs[place],
                    sent.at[place],
                ).start()
    number = 0
    for place, size in enumerate(sizes):
        pltpu.make_async_copy(held.at[pl.ds(number, size)], outs[place], sent.at[place]).wait()
        number += size


def pack(table, sources, groups, after):
    sizes = [sum(count for row, count in group) for group in groups]
    block = sources[0].shape[1:]
    kind = sources[0].dtype
    return pl.pallas_call(
        functools.partial(pack_kernel, groups, len(sources), len(after)),
        out_shape=[jax.ShapeDtypeStruct((size,) + block, kind) for size in sizes],
        in_specs=[SMEM] + [ANY] * (len(sources) + len(after)),
        out_specs=[ANY] * len(groups),
        scratch_shapes=[
            pltpu.VMEM((sum(sizes),) + block, kind),
            pltpu.SemaphoreType.DMA((sum(sizes),)),
            pltpu.SemaphoreType.DMA((len(groups),)),
        ],
        compiler_params=pltpu.CompilerParams(vmem_limit_bytes=VMEM_LIMIT),
        cost_estimate=pl.CostEstimate(flops=0, bytes_accessed=2**16, transcendentals=0),
        name="pack",
    )(table, *sources, *after)


def held_back(x, after):
    def kernel(*refs):
        pass

    return pl.pallas_call(
        kernel,
        out_shape=jax.ShapeDtypeStruct(x.shape, x.dtype),
        in_specs=[ANY] * (1 + len(after)),
        out_specs=ANY,
        input_output_aliases={0: 0},
        cost_estimate=pl.CostEstimate(flops=0, bytes_accessed=0, transcendentals=0),
        name="held_back",
    )(x, *after)


def summed(parts, after):
    def kernel(*refs):
        total = refs[0][...]
        for ref in refs[1:len(parts)]:
            total = total + ref[...]
        refs[-1][...] = total

    x = parts[0]
    whole = pl.BlockSpec(memory_space=pltpu.VMEM)
    return pl.pallas_call(
        kernel,
        out_shape=jax.ShapeDtypeStruct(x.shape, x.dtype),
        in_specs=[whole] * len(parts) + [ANY] * len(after),
        out_specs=whole,
        compiler_params=pltpu.CompilerParams(vmem_limit_bytes=VMEM_LIMIT),
        cost_estimate=pl.CostEstimate(flops=0, bytes_accessed=2**16, transcendentals=0),
        name="summed",
    )(*parts, *after)


def tails(keys, values):
    width = keys.shape[1]
    block = pl.BlockSpec((SPAN, width), lambda i: (keys.shape[0] // SPAN - 1, 0))

    def kernel(k_ref, v_ref, out_ref):
        out_ref[:SPAN] = k_ref[...]
        out_ref[SPAN:] = v_ref[...]

    return pl.pallas_call(
        kernel,
        grid=(1,),
        out_shape=jax.ShapeDtypeStruct((2 * SPAN, width), keys.dtype),
        in_specs=[block, block],
        out_specs=pl.BlockSpec((2 * SPAN, width), lambda i: (0, 0)),
        compiler_params=pltpu.CompilerParams(vmem_limit_bytes=VMEM_LIMIT),
        name="tails",
    )(keys, values)


def plan(block_ids, everyone, heads, blocks_here):
    tok_count = lax.axis_size("tok")
    chips = tok_count // 2
    shard = heads * blocks_here
    here = lax.axis_index("tok")
    chip, core = here // 2, here % 2
    head_of = jnp.arange(heads, dtype=jnp.int32)[None, :, None]
    block = (everyone // blocks_here) * shard + head_of * blocks_here + everyone % blocks_here
    universe = jnp.arange(tok_count * shard, dtype=jnp.int32)
    each = jnp.any(block.reshape(tok_count, -1)[:, :, None] == universe, axis=1)
    need = each.reshape(chips, 2, -1).any(axis=1).reshape(chips, tok_count, shard)
    sibling = lax.dynamic_slice(each, (here ^ 1, here * shard), (1, shard))
    before = jnp.triu(jnp.ones((shard, shard), jnp.bfloat16), 1)

    def ranked(wanted):
        rank = jnp.dot(wanted.astype(jnp.bfloat16), before, preferred_element_type=jnp.float32)
        return jnp.where(wanted, rank.astype(jnp.int32), -1)

    rank = ranked(need)
    count = jnp.sum(need.astype(jnp.int32), axis=2)
    partner = count.reshape(chips, chips, 2)[:, :, ::-1].reshape(count.shape)
    left = jnp.maximum(count - MAIN, 0)
    given = jnp.minimum(jnp.minimum(left, jnp.maximum(MAIN - partner, 0)), HANDED)
    rest = (left - given).reshape(chips, chips, 2)
    ahead = jnp.stack([jnp.zeros_like(rest[..., 0]), rest[..., 0]], axis=2).reshape(count.shape)
    most = jnp.max(jnp.where(jnp.eye(chips, dtype=bool), 0, rest.sum(axis=2)), axis=0)
    core_of = jnp.arange(tok_count, dtype=jnp.int32)[:, None] % 2
    over = rank - MAIN
    is_given = (over >= 0) & (over < given[:, :, None])
    is_second = over >= given[:, :, None]
    turn = over - given[:, :, None] + ahead[:, :, None]
    lane = jnp.where(is_second, turn % 2, jnp.where(is_given, 1 - core_of, core_of))
    spot = jnp.where(is_second, turn // 2, jnp.where(is_given, partner[:, :, None] + over, rank))

    chip_ids = jnp.arange(chips, dtype=jnp.int32)[:, None]
    index = jnp.arange(1, shard + 1, dtype=jnp.int32)

    def of_device(device):
        def cut(x):
            return lax.dynamic_index_in_dim(x, device, 1, keepdims=False)
        live = (cut(rank) >= 0) & (chip_ids != chip)
        return live, cut(is_given), cut(is_second), cut(lane), cut(spot), cut(over)

    def listed(live, spots, size, names):
        slots = jnp.arange(size, dtype=jnp.int32)[None, :, None]
        hit = live[:, None, :] & (spots[:, None, :] == slots)
        return jnp.sum(jnp.where(hit, names[:, None, :], 0), axis=2)

    live, my_given, my_second, my_lane, my_spot, my_over = of_device(here)
    names = jnp.broadcast_to(index, live.shape)
    side = listed(live & my_given, my_over, MAIN, names) - 1
    side_second = listed(live & my_second & (my_lane != core), my_spot, MAIN, names) - 1
    main = listed(live & ~my_second & ~my_given, my_spot, MAIN, names)
    second = listed(live & my_second & (my_lane == core), my_spot, MAIN, names)
    live, sib_given, sib_second, sib_lane, sib_spot, sib_over = of_device(here ^ 1)
    main += listed(live & sib_given, sib_spot, MAIN, KIND + 1 + HANDED * chip_ids + sib_over)
    second += listed(
        live & sib_second & (sib_lane == core), sib_spot, MAIN,
        KIND + 1 + SECOND * chip_ids + sib_spot,
    )
    beside = listed(ranked(sibling) >= 0, ranked(sibling), MAIN, index[None, :])
    main = jnp.where(chip_ids == chip, beside, main) - 1
    table = jnp.concatenate([side, main, side_second, second - 1])
    sender = jnp.arange(tok_count, dtype=jnp.int32)[:, None]
    to_me = [lax.dynamic_index_in_dim(x, chip, 0, keepdims=False) for x in (is_second, lane, spot)]
    away = (to_me[1] != core).astype(jnp.int32)
    place = jnp.where(
        to_me[0], (3 + away) * KIND + to_me[2],
        (1 + away) * KIND + MAIN * (sender // 2) + to_me[2],
    )
    mine = ranked(lax.dynamic_slice(each, (here, (here ^ 1) * shard), (1, shard)))
    place = jnp.where(sender == here, jnp.arange(shard, dtype=jnp.int32), place)
    place = jnp.where(sender == here ^ 1, 2 * KIND + MAIN * chip + mine, place).reshape(-1)
    own = (block_ids // blocks_here) * shard + head_of * blocks_here + block_ids % blocks_here
    loc = jnp.sum(jnp.where(own.reshape(-1, 1) == universe, place, 0), axis=1)
    loc = loc.reshape(block_ids.shape)
    waits = jnp.any(loc >= 3 * KIND, axis=(0, 2))
    ready = jnp.min(jnp.where(waits, jnp.arange(heads), heads - 1))
    return table, loc, most, ready


def between_chips(block):
    count = lax.axis_size("tok")
    groups = [[i for i in range(count) if i % 2 == core] for core in range(2)]
    return lax.all_to_all(
        block, "tok", split_axis=0, concat_axis=0, axis_index_groups=groups, tiled=True
    )


def chip_shift(block, source, distance):
    count = lax.axis_size("tok")
    route = [(i, (i + 2 * distance) % count) for i in (2 * source, 2 * source + 1)]
    return lax.ppermute(block, "tok", route)


def core_swap(block):
    return lax.ppermute(block, "tok", [(i, i ^ 1) for i in range(lax.axis_size("tok"))])


def most_of_all(most):
    count = lax.axis_size("mem")
    step = 1
    while step < count:
        other = lax.ppermute(most, "mem", [(i, i ^ step) for i in range(count)])
        most = jnp.maximum(most, other)
        step *= 2
    return most


def per_device(queries, keys, values, memory, block_ids, gate_bias, grad_out):
    my_rank = lax.axis_index("tok")
    tok_count = lax.axis_size("tok")
    heads, blocks_here = memory.shape[:2]
    chips = tok_count // 2
    direct = chips == 4 and lax.axis_size("mem") == 4
    gates = jax.nn.sigmoid(gate_bias)
    prev_ok = (my_rank > 0).astype(jnp.int32).reshape(1)
    if direct:
        everyone = lax.all_to_all(
            jnp.broadcast_to(block_ids[None], (tok_count,) + block_ids.shape),
            "tok", split_axis=0, concat_axis=0, tiled=True,
        )
    tail = tails(keys, values)
    halo = passed_along(tail, "tok", 1)
    carry, token = (), ()
    if direct:
        near = memory.reshape(-1, BLOCK, memory.shape[-1])
        table, loc, most, ready = plan(block_ids, everyone, heads, blocks_here)
        (side,) = pack(
            table, [near], [[(chip, HANDED) for chip in range(chips)]], (tail,)
        )
        handed = core_swap(side)
        (main,) = pack(
            table, [near, handed], [[(chips + chip, MAIN) for chip in range(chips)]], ()
        )
        own_main = between_chips(main)
        (side,) = pack(
            table, [near], [[(2 * chips + chip, SECOND) for chip in range(chips)]], (main,)
        )
        handed = core_swap(side)
        token = (side,)
    for head in range(heads):
        if direct and head == 4:
            token = token + (loc, most)
        carry, token = local_head(
            head, gates, prev_ok, queries, keys, values, grad_out, halo, carry, token
        )
        if direct and head == 1:
            most = jnp.broadcast_to(jnp.pad(most, (0, 8 - chips))[:, None], (8, 128))
            most = most_of_all(most + token.astype(jnp.int32))
            hot = jnp.argmax(most[:chips, 0]).astype(jnp.int32)
            limit = jnp.where(jnp.arange(chips) == hot, 2 * SECOND, 0)
            overflow = jnp.any(most[:chips, 0] > limit)
            branch = jnp.where(overflow, chips, hot)
        token = (token,)

    def finish(start, stop, where, sources, made):
        return memory_heads(
            start, stop, where, gates, queries, grad_out, carry, sources, made
        )

    def full_exchange():
        returned, where = exchange_all(memory, block_ids)
        return tuple(finish(0, heads, where, [returned], ())[:2])

    back = passed_along(carry[6], "tok", -1)
    if not direct:
        out, dq = full_exchange()
        return out, dq, *close_grads(carry, back, block_ids)

    def from_chip(source):
        def send():
            late = [chip_shift(seconds[(source + k) % chips], source, k) for k in range(1, chips)]
            sources = [near, own_main, core_swap(own_main)]
            *made, made_token = finish(0, ready, loc, sources, ())
            late = summed(late, (made_token,))
            sources += [late, core_swap(late)]
            out, dq, _ = finish(ready, heads, loc, sources, made)
            return out, dq
        return send

    seconds = pack(
        table, [near, handed], [[(3 * chips + chip, SECOND)] for chip in range(chips)], token
    )
    own_main = held_back(own_main, seconds)
    out, dq = lax.switch(
        branch, [from_chip(source) for source in range(chips)] + [full_exchange]
    )
    dk, dv = close_grads(carry, back, out)
    return out, dq, dk, dv


def solution(mesh):
    in_specs = (
        P("tok", "mem"),
        P("tok", "mem"),
        P("tok", "mem"),
        P("mem", "tok", None, None),
        P("tok", "mem", None),
        P("mem"),
        P("tok", "mem"),
    )
    out_specs = (P("tok", "mem"), P("tok", "mem"), P("tok", "mem"), P("tok", "mem"))
    return jax.shard_map(
        per_device, mesh=mesh, in_specs=in_specs, out_specs=out_specs, check_vma=False
    )
```

```python
import functools

import jax
import jax.numpy as jnp
from jax import lax
from jax.experimental import pallas as pl
from jax.experimental.pallas import tpu as pltpu
from jax.sharding import PartitionSpec as P

SPAN = 512
HALF = 256
BLOCK = 128
R = 4
HD = 128
NEG = -1e30
LOG2E = 1.4426950408889634
KIND = 512
VMEM_LIMIT = 56 * 2**20
MAIN = 19
HANDED = 5
SECOND = 6
ANY = pl.BlockSpec(memory_space=pl.ANY)
SMEM = pl.BlockSpec(memory_space=pltpu.SMEM)


def passed_along(block, axis, distance):
    devices = range(lax.axis_size(axis))
    route = [(i - distance, i) for i in devices if i - distance in devices]
    return lax.ppermute(block, axis, route)


def mm(a, b, dims):
    return lax.dot_general(a, b, (dims, ((), ())), preferred_element_type=jnp.float32)


def local_kernel(head, n_any, gates, prev_ok, q_ref, k_ref, v_ref, g_ref, halo_ref, *rest):
    (lo_ref, dq_ref, dk_ref, dv_ref, dkx_ref, dvx_ref, back_k_ref, back_v_ref, token_ref,
     kx, vx, kt, vt, acc_k, acc_v) = rest[n_any:]
    scaling = HD ** -0.5
    keep = 1.0 - gates[head]
    kx[:SPAN] = halo_ref[:SPAN]
    kx[SPAN:] = k_ref[...]
    vx[:SPAN] = halo_ref[SPAN:]
    vx[SPAN:] = v_ref[...]
    kt[...] = kx[...].T
    vt[...] = vx[...].T
    ok = prev_ok[0] > 0
    tri = (lax.broadcasted_iota(jnp.int32, (HALF, HALF), 0)
           <= lax.broadcasted_iota(jnp.int32, (HALF, HALF), 1))
    for span in range(2):
        for half in range(2):
            row0 = span * SPAN + half * HALF
            win0 = span * SPAN
            width = SPAN + HALF * (half + 1)
            rows = pl.ds(row0, HALF)
            win = pl.ds(win0, width)
            q = q_ref[rows, :]
            gl = (keep * g_ref[rows, :].astype(jnp.float32)).astype(jnp.bfloat16)
            st = mm(kx[win, :], q, ((1,), (1,))) * scaling
            first = st[:SPAN]
            if span == 0:
                first = jnp.where(ok, first, NEG)
            parts = [first]
            if half:
                parts.append(st[SPAN:width - HALF])
            parts.append(jnp.where(tri, st[width - HALF:], NEG))
            st = jnp.concatenate(parts, axis=0)
            top = jnp.max(st, axis=0, keepdims=True)
            e = jnp.exp(st - top)
            total = jnp.sum(e, axis=0, keepdims=True)
            pt = (e * (1.0 / total)).astype(jnp.bfloat16)
            out_t = mm(vt[:, win], pt, ((1,), (0,)))
            gt = gl.astype(jnp.float32).T
            dot = jnp.sum(gt * out_t, axis=0, keepdims=True)
            dpt = mm(vx[win, :], gl, ((1,), (1,)))
            dst = (pt.astype(jnp.float32) * (dpt - dot)).astype(jnp.bfloat16)
            dq_t = mm(kt[:, win], dst, ((1,), (0,)))
            lo_ref[rows, :] = keep * out_t.T
            dq_ref[rows, :] = scaling * dq_t.T
            dkw = mm(dst, q, ((1,), (0,)))
            dvw = mm(pt, gl, ((1,), (0,)))
            if span == 0 and half == 0:
                acc_k[win, :] = dkw
                acc_v[win, :] = dvw
            else:
                old = 768 if span == 0 else (1024 if half == 0 else 1280)
                seen = max(0, min(old, win0 + width) - win0)
                acc_k[pl.ds(win0, seen), :] += dkw[:seen]
                acc_v[pl.ds(win0, seen), :] += dvw[:seen]
                if seen < width:
                    acc_k[pl.ds(win0 + seen, width - seen), :] = dkw[seen:]
                    acc_v[pl.ds(win0 + seen, width - seen), :] = dvw[seen:]
    back_k_ref[...] = (scaling * acc_k[:SPAN]).astype(jnp.bfloat16)
    back_v_ref[...] = acc_v[:SPAN].astype(jnp.bfloat16)
    dk_ref[...] = (scaling * acc_k[SPAN:2 * SPAN]).astype(jnp.bfloat16)
    dv_ref[...] = acc_v[SPAN:2 * SPAN].astype(jnp.bfloat16)
    dkx_ref[...] = scaling * acc_k[2 * SPAN:]
    dvx_ref[...] = acc_v[2 * SPAN:]
    token_ref[...] = jnp.zeros_like(token_ref)


def local_head(head, gates, prev_ok, q, k, v, g, halo, carry, after):
    rows, width = q.shape
    col = pl.BlockSpec((rows, HD), lambda i: (0, head))
    col_half = pl.BlockSpec((SPAN, HD), lambda i: (0, head))
    shapes = [
        jax.ShapeDtypeStruct((rows, width), jnp.float32),
        jax.ShapeDtypeStruct((rows, width), jnp.float32),
        jax.ShapeDtypeStruct((rows, width), jnp.bfloat16),
        jax.ShapeDtypeStruct((rows, width), jnp.bfloat16),
        jax.ShapeDtypeStruct((SPAN, width), jnp.float32),
        jax.ShapeDtypeStruct((SPAN, width), jnp.float32),
        jax.ShapeDtypeStruct((SPAN, width), jnp.bfloat16),
        jax.ShapeDtypeStruct((SPAN, width), jnp.bfloat16),
        jax.ShapeDtypeStruct((8, 128), jnp.float32),
    ]
    extra = list(carry) + list(after)
    result = pl.pallas_call(
        functools.partial(local_kernel, head, len(extra)),
        grid=(1,),
        out_shape=shapes,
        in_specs=[SMEM, SMEM, col, col, col, col, col] + [ANY] * len(extra),
        out_specs=[col, col, col_half, col_half, col_half, col_half, col_half, col_half,
                   pl.BlockSpec((8, 128), lambda i: (0, 0))],
        scratch_shapes=[
            pltpu.VMEM((3 * SPAN, HD), jnp.bfloat16),
            pltpu.VMEM((3 * SPAN, HD), jnp.bfloat16),
            pltpu.VMEM((HD, 3 * SPAN), jnp.bfloat16),
            pltpu.VMEM((HD, 3 * SPAN), jnp.bfloat16),
            pltpu.VMEM((3 * SPAN, HD), jnp.float32),
            pltpu.VMEM((3 * SPAN, HD), jnp.float32),
        ],
        input_output_aliases={7 + i: i for i in range(len(carry))},
        compiler_params=pltpu.CompilerParams(vmem_limit_bytes=VMEM_LIMIT),
        cost_estimate=pl.CostEstimate(flops=9 * 10**9, bytes_accessed=4 * 2**20,
                                      transcendentals=2 * 512 * 896),
        name="local_head",
    )(gates, prev_ok, q, k, v, g, halo, *extra)
    return result[:8], result[8]


def memory_kernel(n_src, n_any, bounds, loc, gates, q_ref, g_ref, lo_ref, dqf_ref, *rest):
    sources = rest[:n_src]
    out_ref, dq_ref, token_ref, buf, sems = rest[n_src + n_any:]
    token_ref[...] = jnp.zeros_like(token_ref)
    head = pl.program_id(0)
    start, stop = bounds[0], bounds[1]
    scaling = HD ** -0.5

    def fetch(h, slot):
        for j in range(2 * R):
            code = loc[j // R, h, j % R]
            kind, index = code // KIND, lax.rem(code, KIND)

            def pick(low, high):
                if high - low == 1:
                    pltpu.make_async_copy(
                        sources[low].at[index], buf.at[slot, j], sems.at[slot, j]
                    ).start()
                    return
                middle = (low + high) // 2

                @pl.when(kind < middle)
                def _():
                    pick(low, middle)

                @pl.when(kind >= middle)
                def _():
                    pick(middle, high)

            pick(0, n_src)

    @pl.when((head == 0) & (start < stop))
    def _():
        fetch(start, lax.rem(start, 2))

    @pl.when((head >= start) & (head < stop))
    def _():
        slot = lax.rem(head, 2)

        @pl.when(head + 1 < stop)
        def _():
            fetch(head + 1, 1 - slot)

        for j in range(2 * R):
            pltpu.make_async_copy(sources[0].at[0], buf.at[slot, j], sems.at[slot, j]).wait()
        gate = gates[head]
        for span in range(2):
            blocks = buf[slot, pl.ds(span * R, R)]
            mk = blocks[:, :, :HD].reshape(R * BLOCK, HD)
            mv = blocks[:, :, HD:].reshape(R * BLOCK, HD)
            rows = pl.ds(span * SPAN, SPAN)
            q = q_ref[rows, :]
            gm = (gate * g_ref[rows, :].astype(jnp.float32)).astype(jnp.bfloat16)
            s = mm(q, mk, ((1,), (1,)))
            top = jnp.max(s, axis=1, keepdims=True)
            e = jnp.exp2((s - top) * (scaling * LOG2E))
            share = 1.0 / jnp.sum(e, axis=1, keepdims=True)
            mo = mm(e.astype(jnp.bfloat16), mv, ((1,), (0,))) * share
            dp = mm(gm, mv, ((1,), (1,)))
            dot = jnp.sum(gm.astype(jnp.float32) * mo, axis=1, keepdims=True)
            ds = (e * (dp - dot)).astype(jnp.bfloat16)
            dqm = mm(ds, mk, ((1,), (0,))) * (share * scaling)
            out_ref[rows, :] = (gate * mo + lo_ref[rows, :]).astype(jnp.bfloat16)
            dq_ref[rows, :] = (dqm + dqf_ref[rows, :]).astype(jnp.bfloat16)


def memory_heads(start, stop, loc, gates, q, g, carry, sources, made, after=()):
    rows, width = q.shape
    heads = width // HD
    bounds = jnp.stack([jnp.int32(start), jnp.int32(stop)])

    def column(h, bounds):
        return 0, jnp.clip(h, bounds[0], jnp.maximum(bounds[1] - 1, bounds[0]))

    col = pl.BlockSpec((rows, HD), column)
    full = jax.ShapeDtypeStruct((rows, width), jnp.bfloat16)
    extra = list(made) + list(after)
    return pl.pallas_call(
        functools.partial(memory_kernel, len(sources), len(extra)),
        grid_spec=pltpu.PrefetchScalarGridSpec(
            num_scalar_prefetch=1,
            grid=(heads,),
            in_specs=[SMEM, SMEM, col, col, col, col] + [ANY] * (len(sources) + len(extra)),
            out_specs=[col, col, pl.BlockSpec((16, 128), lambda h, bounds: (0, 0))],
            scratch_shapes=[
                pltpu.VMEM((2, 2 * R, BLOCK, 2 * HD), jnp.bfloat16),
                pltpu.SemaphoreType.DMA((2, 2 * R)),
            ],
        ),
        out_shape=[full, full, jax.ShapeDtypeStruct((16, 128), jnp.bfloat16)],
        input_output_aliases={7 + len(sources) + i: i for i in range(len(made))},
        compiler_params=pltpu.CompilerParams(vmem_limit_bytes=VMEM_LIMIT),
        cost_estimate=pl.CostEstimate(flops=14 * 10**9, bytes_accessed=2**20,
                                      transcendentals=heads * 2 * 512 * 512),
        name="memory_heads",
    )(bounds, loc, gates, q, g, carry[0], carry[1], *sources, *extra)


def close_kernel(dkx_ref, dvx_ref, bk_ref, bv_ref, dk_in, dv_in, after_ref, dk_ref, dv_ref):
    dk_ref[...] = (dkx_ref[...] + bk_ref[...].astype(jnp.float32)).astype(jnp.bfloat16)
    dv_ref[...] = (dvx_ref[...] + bv_ref[...].astype(jnp.float32)).astype(jnp.bfloat16)


def close_grads(carry, back_k, back_v, after):
    dk, dv, dkx, dvx = carry[2:6]
    width = dk.shape[1]
    part = width // 4
    upper = pl.BlockSpec((SPAN, part), lambda h: (0, h))
    lower = pl.BlockSpec((SPAN, part), lambda h: (1, h))
    return pl.pallas_call(
        close_kernel,
        grid=(4,),
        out_shape=[jax.ShapeDtypeStruct(dk.shape, dk.dtype)] * 2,
        in_specs=[upper] * 4 + [ANY] * 3,
        out_specs=[lower, lower],
        input_output_aliases={4: 0, 5: 1},
        compiler_params=pltpu.CompilerParams(vmem_limit_bytes=VMEM_LIMIT),
        name="close_grads",
    )(dkx, dvx, back_k, back_v, dk, dv, after)


def exchange_all(memory, block_ids):
    tok_count = lax.axis_size("tok")
    heads_here, blocks_here = memory.shape[:2]
    wanted = block_ids.reshape(-1)
    request_count = wanted.shape[0]
    owner_rank = wanted // blocks_here
    head_index = jnp.arange(request_count) // R % heads_here
    request_code = head_index * blocks_here + wanted % blocks_here
    order_ids = jnp.arange(request_count)
    same_owner = owner_rank[:, None] == owner_rank[None, :]
    slot_index = jnp.sum(same_owner & (order_ids[None, :] < order_ids[:, None]), axis=1)
    capacity = 2 * request_count // tok_count
    to_owner = (owner_rank[:, None] == jnp.arange(tok_count)[None, :]).astype(jnp.int32)
    to_slot = (slot_index[:, None] == jnp.arange(capacity)[None, :]).astype(jnp.int32)
    request_table = jnp.sum(
        request_code[:, None, None] * to_owner[:, :, None] * to_slot[:, None, :], axis=0
    )
    mem_flat = memory.reshape(-1, BLOCK, memory.shape[-1])
    found = mem_flat[lax.all_to_all(request_table, "tok", split_axis=0, concat_axis=0, tiled=True)]
    returned = lax.all_to_all(found, "tok", split_axis=0, concat_axis=0, tiled=True)
    loc = (owner_rank * capacity + slot_index).reshape(block_ids.shape)
    return returned.reshape(-1, BLOCK, memory.shape[-1]), loc.astype(jnp.int32)


def pack_kernel(groups, n_src, n_any, table, *rest):
    sources = rest[:n_src]
    outs = rest[n_src + n_any:n_src + n_any + len(groups)]
    held, sems, sent = rest[-3:]
    sizes = [sum(count for row, count in group) for group in groups]
    for phase in range(2):
        number = 0
        for place, group in enumerate(groups):
            for row, count in group:
                for j in range(count):
                    code = table[row, j]
                    for kind, source in enumerate(sources):
                        @pl.when((code >= kind * KIND) & (code < (kind + 1) * KIND))
                        def _():
                            copy = pltpu.make_async_copy(
                                source.at[code - kind * KIND], held.at[number], sems.at[number]
                            )
                            copy.wait() if phase else copy.start()
                    number += 1
            if phase:
                pltpu.make_async_copy(
                    held.at[pl.ds(number - sizes[place], sizes[place])], outs[place],
                    sent.at[place],
                ).start()
    number = 0
    for place, size in enumerate(sizes):
        pltpu.make_async_copy(held.at[pl.ds(number, size)], outs[place], sent.at[place]).wait()
        number += size


def pack(table, sources, groups, after):
    sizes = [sum(count for row, count in group) for group in groups]
    block = sources[0].shape[1:]
    kind = sources[0].dtype
    return pl.pallas_call(
        functools.partial(pack_kernel, groups, len(sources), len(after)),
        out_shape=[jax.ShapeDtypeStruct((size,) + block, kind) for size in sizes],
        in_specs=[SMEM] + [ANY] * (len(sources) + len(after)),
        out_specs=[ANY] * len(groups),
        scratch_shapes=[
            pltpu.VMEM((sum(sizes),) + block, kind),
            pltpu.SemaphoreType.DMA((sum(sizes),)),
            pltpu.SemaphoreType.DMA((len(groups),)),
        ],
        compiler_params=pltpu.CompilerParams(vmem_limit_bytes=VMEM_LIMIT),
        cost_estimate=pl.CostEstimate(flops=0, bytes_accessed=2**16, transcendentals=0),
        name="pack",
    )(table, *sources, *after)


def held_back(x, after):
    def kernel(*refs):
        pass

    return pl.pallas_call(
        kernel,
        out_shape=jax.ShapeDtypeStruct(x.shape, x.dtype),
        in_specs=[ANY] * (1 + len(after)),
        out_specs=ANY,
        input_output_aliases={0: 0},
        cost_estimate=pl.CostEstimate(flops=0, bytes_accessed=0, transcendentals=0),
        name="held_back",
    )(x, *after)


def summed(parts, after):
    def kernel(*refs):
        total = refs[0][...]
        for ref in refs[1:len(parts)]:
            total = total + ref[...]
        refs[-1][...] = total

    x = parts[0]
    whole = pl.BlockSpec(memory_space=pltpu.VMEM)
    return pl.pallas_call(
        kernel,
        out_shape=jax.ShapeDtypeStruct(x.shape, x.dtype),
        in_specs=[whole] * len(parts) + [ANY] * len(after),
        out_specs=whole,
        compiler_params=pltpu.CompilerParams(vmem_limit_bytes=VMEM_LIMIT),
        cost_estimate=pl.CostEstimate(flops=0, bytes_accessed=2**16, transcendentals=0),
        name="summed",
    )(*parts, *after)


def tails(keys, values):
    width = keys.shape[1]
    block = pl.BlockSpec((SPAN, width), lambda i: (keys.shape[0] // SPAN - 1, 0))

    def kernel(k_ref, v_ref, out_ref):
        out_ref[:SPAN] = k_ref[...]
        out_ref[SPAN:] = v_ref[...]

    return pl.pallas_call(
        kernel,
        grid=(1,),
        out_shape=jax.ShapeDtypeStruct((2 * SPAN, width), keys.dtype),
        in_specs=[block, block],
        out_specs=pl.BlockSpec((2 * SPAN, width), lambda i: (0, 0)),
        compiler_params=pltpu.CompilerParams(vmem_limit_bytes=VMEM_LIMIT),
        name="tails",
    )(keys, values)


def plan(block_ids, everyone, heads, blocks_here):
    tok_count = lax.axis_size("tok")
    chips = tok_count // 2
    shard = heads * blocks_here
    here = lax.axis_index("tok")
    chip, core = here // 2, here % 2
    head_of = jnp.arange(heads, dtype=jnp.int32)[None, :, None]
    block = (everyone // blocks_here) * shard + head_of * blocks_here + everyone % blocks_here
    universe = jnp.arange(tok_count * shard, dtype=jnp.int32)
    each = jnp.any(block.reshape(tok_count, -1)[:, :, None] == universe, axis=1)
    need = each.reshape(chips, 2, -1).any(axis=1).reshape(chips, tok_count, shard)
    sibling = lax.dynamic_slice(each, (here ^ 1, here * shard), (1, shard))
    before = jnp.triu(jnp.ones((shard, shard), jnp.bfloat16), 1)

    def ranked(wanted):
        rank = jnp.dot(wanted.astype(jnp.bfloat16), before, preferred_element_type=jnp.float32)
        return jnp.where(wanted, rank.astype(jnp.int32), -1)

    rank = ranked(need)
    count = jnp.sum(need.astype(jnp.int32), axis=2)
    partner = count.reshape(chips, chips, 2)[:, :, ::-1].reshape(count.shape)
    left = jnp.maximum(count - MAIN, 0)
    given = jnp.minimum(jnp.minimum(left, jnp.maximum(MAIN - partner, 0)), HANDED)
    rest = (left - given).reshape(chips, chips, 2)
    ahead = jnp.stack([jnp.zeros_like(rest[..., 0]), rest[..., 0]], axis=2).reshape(count.shape)
    most = jnp.max(jnp.where(jnp.eye(chips, dtype=bool), 0, rest.sum(axis=2)), axis=0)
    core_of = jnp.arange(tok_count, dtype=jnp.int32)[:, None] % 2
    over = rank - MAIN
    is_given = (over >= 0) & (over < given[:, :, None])
    is_second = over >= given[:, :, None]
    turn = over - given[:, :, None] + ahead[:, :, None]
    lane = jnp.where(is_second, turn % 2, jnp.where(is_given, 1 - core_of, core_of))
    spot = jnp.where(is_second, turn // 2, jnp.where(is_given, partner[:, :, None] + over, rank))

    chip_ids = jnp.arange(chips, dtype=jnp.int32)[:, None]
    index = jnp.arange(1, shard + 1, dtype=jnp.int32)

    def of_device(device):
        def cut(x):
            return lax.dynamic_index_in_dim(x, device, 1, keepdims=False)
        live = (cut(rank) >= 0) & (chip_ids != chip)
        return live, cut(is_given), cut(is_second), cut(lane), cut(spot), cut(over)

    def listed(live, spots, size, names):
        slots = jnp.arange(size, dtype=jnp.int32)[None, :, None]
        hit = live[:, None, :] & (spots[:, None, :] == slots)
        return jnp.sum(jnp.where(hit, names[:, None, :], 0), axis=2)

    live, my_given, my_second, my_lane, my_spot, my_over = of_device(here)
    names = jnp.broadcast_to(index, live.shape)
    side = listed(live & my_given, my_over, MAIN, names) - 1
    side_second = listed(live & my_second & (my_lane != core), my_spot, MAIN, names) - 1
    main = listed(live & ~my_second & ~my_given, my_spot, MAIN, names)
    second = listed(live & my_second & (my_lane == core), my_spot, MAIN, names)
    live, sib_given, sib_second, sib_lane, sib_spot, sib_over = of_device(here ^ 1)
    main += listed(live & sib_given, sib_spot, MAIN, KIND + 1 + HANDED * chip_ids + sib_over)
    second += listed(
        live & sib_second & (sib_lane == core), sib_spot, MAIN,
        KIND + 1 + SECOND * chip_ids + sib_spot,
    )
    beside = listed(ranked(sibling) >= 0, ranked(sibling), MAIN, index[None, :])
    main = jnp.where(chip_ids == chip, beside, main) - 1
    table = jnp.concatenate([side, main, side_second, second - 1])
    sender = jnp.arange(tok_count, dtype=jnp.int32)[:, None]
    to_me = [lax.dynamic_index_in_dim(x, chip, 0, keepdims=False) for x in (is_second, lane, spot)]
    away = (to_me[1] != core).astype(jnp.int32)
    place = jnp.where(
        to_me[0], (3 + away) * KIND + to_me[2],
        (1 + away) * KIND + MAIN * (sender // 2) + to_me[2],
    )
    mine = ranked(lax.dynamic_slice(each, (here, (here ^ 1) * shard), (1, shard)))
    place = jnp.where(sender == here, jnp.arange(shard, dtype=jnp.int32), place)
    place = jnp.where(sender == here ^ 1, 2 * KIND + MAIN * chip + mine, place).reshape(-1)
    own = (block_ids // blocks_here) * shard + head_of * blocks_here + block_ids % blocks_here
    loc = jnp.sum(jnp.where(own.reshape(-1, 1) == universe, place, 0), axis=1)
    loc = loc.reshape(block_ids.shape)
    waits = jnp.any(loc >= 3 * KIND, axis=(0, 2))
    ready = jnp.min(jnp.where(waits, jnp.arange(heads), heads - 1))
    return table, loc, most, ready


def between_chips(block):
    count = lax.axis_size("tok")
    groups = [[i for i in range(count) if i % 2 == core] for core in range(2)]
    return lax.all_to_all(
        block, "tok", split_axis=0, concat_axis=0, axis_index_groups=groups, tiled=True
    )


def chip_shift(block, source, distance):
    count = lax.axis_size("tok")
    route = [(i, (i + 2 * distance) % count) for i in (2 * source, 2 * source + 1)]
    return lax.ppermute(block, "tok", route)


def core_swap(block):
    return lax.ppermute(block, "tok", [(i, i ^ 1) for i in range(lax.axis_size("tok"))])


def most_of_all(most):
    count = lax.axis_size("mem")
    step = 1
    while step < count:
        other = lax.ppermute(most, "mem", [(i, i ^ step) for i in range(count)])
        most = jnp.maximum(most, other)
        step *= 2
    return most


def per_device(queries, keys, values, memory, block_ids, gate_bias, grad_out):
    my_rank = lax.axis_index("tok")
    tok_count = lax.axis_size("tok")
    heads, blocks_here = memory.shape[:2]
    chips = tok_count // 2
    direct = chips == 4 and lax.axis_size("mem") == 4
    gates = jax.nn.sigmoid(gate_bias)
    prev_ok = (my_rank > 0).astype(jnp.int32).reshape(1)
    if direct:
        everyone = lax.all_to_all(
            jnp.broadcast_to(block_ids[None], (tok_count,) + block_ids.shape),
            "tok", split_axis=0, concat_axis=0, tiled=True,
        )
    tail = tails(keys, values)
    halo = passed_along(tail, "tok", 1)
    carry, token = (), ()
    if direct:
        near = memory.reshape(-1, BLOCK, memory.shape[-1])
        table, loc, most, ready = plan(block_ids, everyone, heads, blocks_here)
        (side,) = pack(
            table, [near], [[(chip, HANDED) for chip in range(chips)]], (tail,)
        )
        handed = core_swap(side)
        (main,) = pack(
            table, [near, handed], [[(chips + chip, MAIN) for chip in range(chips)]], ()
        )
        own_main = between_chips(main)
        (side,) = pack(
            table, [near], [[(2 * chips + chip, SECOND) for chip in range(chips)]], (main,)
        )
        handed = core_swap(side)
        token = (side,)
    for head in range(heads):
        if direct and head == 4:
            token = token + (loc, most)
        carry, token = local_head(
            head, gates, prev_ok, queries, keys, values, grad_out, halo, carry, token
        )
        if direct and head == 1:
            most = jnp.broadcast_to(jnp.pad(most, (0, 8 - chips))[:, None], (8, 128))
            most = most_of_all(most + token.astype(jnp.int32))
            hot = jnp.argmax(most[:chips, 0]).astype(jnp.int32)
            limit = jnp.where(jnp.arange(chips) == hot, 2 * SECOND, 0)
            overflow = jnp.any(most[:chips, 0] > limit)
            branch = jnp.where(overflow, chips, hot)
        token = (token,)

    def finish(start, stop, where, sources, made):
        return memory_heads(
            start, stop, where, gates, queries, grad_out, carry, sources, made
        )

    def full_exchange(halo_grad):
        returned, where = exchange_all(memory, block_ids)
        out, dq, _ = finish(0, heads, where, [returned], ())
        return out, dq, passed_along(halo_grad, "tok", -1)

    back_k = passed_along(carry[6], "tok", -1)
    if not direct:
        out, dq, back_v = full_exchange(carry[7])
        return out, dq, *close_grads(carry, back_k, back_v, block_ids)

    def from_chip(source):
        def send(halo_grad):
            late = [chip_shift(seconds[(source + k) % chips], source, k) for k in range(1, chips)]
            back = passed_along(halo_grad, "tok", -1)
            sources = [near, own_main, core_swap(own_main)]
            *made, made_token = finish(0, ready, loc, sources, ())
            late = summed(late, (made_token,))
            sources += [late, core_swap(late)]
            out, dq, _ = finish(ready, heads, loc, sources, made)
            return out, dq, back
        return send

    seconds = pack(
        table, [near, handed], [[(3 * chips + chip, SECOND)] for chip in range(chips)], token
    )
    own_main = held_back(own_main, seconds)
    out, dq, back_v = lax.switch(
        branch, [from_chip(source) for source in range(chips)] + [full_exchange], carry[7]
    )
    dk, dv = close_grads(carry, back_k, back_v, out)
    return out, dq, dk, dv


def solution(mesh):
    in_specs = (
        P("tok", "mem"),
        P("tok", "mem"),
        P("tok", "mem"),
        P("mem", "tok", None, None),
        P("tok", "mem", None),
        P("mem"),
        P("tok", "mem"),
    )
    out_specs = (P("tok", "mem"), P("tok", "mem"), P("tok", "mem"), P("tok", "mem"))
    return jax.shard_map(
        per_device, mesh=mesh, in_specs=in_specs, out_specs=out_specs, check_vma=False
    )
```

```python
import functools

import jax
import jax.numpy as jnp
from jax import lax
from jax.experimental import pallas as pl
from jax.experimental.pallas import tpu as pltpu
from jax.sharding import PartitionSpec as P

SPAN = 512
HALF = 256
BLOCK = 128
R = 4
HD = 128
NEG = -1e30
LOG2E = 1.4426950408889634
KIND = 512
VMEM_LIMIT = 56 * 2**20
MAIN = 19
HANDED = 5
SECOND = 6
REST = 256
ANY = pl.BlockSpec(memory_space=pl.ANY)
SMEM = pl.BlockSpec(memory_space=pltpu.SMEM)


def passed_along(block, axis, distance):
    devices = range(lax.axis_size(axis))
    route = [(i - distance, i) for i in devices if i - distance in devices]
    return lax.ppermute(block, axis, route)


def mm(a, b, dims):
    return lax.dot_general(a, b, (dims, ((), ())), preferred_element_type=jnp.float32)


def local_kernel(head, n_any, gates, prev_ok, q_ref, k_ref, v_ref, g_ref, halo_ref, *rest):
    (lo_ref, dq_ref, dk_ref, dv_ref, dkx_ref, dvx_ref, back_k_ref, back_v_ref, token_ref,
     kx, vx, kt, vt, acc_k, acc_v) = rest[n_any:]
    scaling = HD ** -0.5
    keep = 1.0 - gates[head]
    kx[:SPAN] = halo_ref[:SPAN]
    kx[SPAN:] = k_ref[...]
    vx[:SPAN] = halo_ref[SPAN:]
    vx[SPAN:] = v_ref[...]
    kt[...] = kx[...].T
    vt[...] = vx[...].T
    ok = prev_ok[0] > 0
    tri = (lax.broadcasted_iota(jnp.int32, (HALF, HALF), 0)
           <= lax.broadcasted_iota(jnp.int32, (HALF, HALF), 1))
    for span in range(2):
        for half in range(2):
            row0 = span * SPAN + half * HALF
            win0 = span * SPAN
            width = SPAN + HALF * (half + 1)
            rows = pl.ds(row0, HALF)
            win = pl.ds(win0, width)
            q = q_ref[rows, :]
            gl = (keep * g_ref[rows, :].astype(jnp.float32)).astype(jnp.bfloat16)
            st = mm(kx[win, :], q, ((1,), (1,))) * scaling
            first = st[:SPAN]
            if span == 0:
                first = jnp.where(ok, first, NEG)
            parts = [first]
            if half:
                parts.append(st[SPAN:width - HALF])
            parts.append(jnp.where(tri, st[width - HALF:], NEG))
            st = jnp.concatenate(parts, axis=0)
            top = jnp.max(st, axis=0, keepdims=True)
            e = jnp.exp(st - top)
            total = jnp.sum(e, axis=0, keepdims=True)
            pt = (e * (1.0 / total)).astype(jnp.bfloat16)
            out_t = mm(vt[:, win], pt, ((1,), (0,)))
            gt = gl.astype(jnp.float32).T
            dot = jnp.sum(gt * out_t, axis=0, keepdims=True)
            dpt = mm(vx[win, :], gl, ((1,), (1,)))
            dst = (pt.astype(jnp.float32) * (dpt - dot)).astype(jnp.bfloat16)
            dq_t = mm(kt[:, win], dst, ((1,), (0,)))
            lo_ref[rows, :] = keep * out_t.T
            dq_ref[rows, :] = scaling * dq_t.T
            dkw = mm(dst, q, ((1,), (0,)))
            dvw = mm(pt, gl, ((1,), (0,)))
            if span == 0 and half == 0:
                acc_k[win, :] = dkw
                acc_v[win, :] = dvw
            else:
                old = 768 if span == 0 else (1024 if half == 0 else 1280)
                seen = max(0, min(old, win0 + width) - win0)
                acc_k[pl.ds(win0, seen), :] += dkw[:seen]
                acc_v[pl.ds(win0, seen), :] += dvw[:seen]
                if seen < width:
                    acc_k[pl.ds(win0 + seen, width - seen), :] = dkw[seen:]
                    acc_v[pl.ds(win0 + seen, width - seen), :] = dvw[seen:]
    back_k_ref[:SPAN] = (scaling * acc_k[:SPAN]).astype(jnp.bfloat16)
    back_k_ref[SPAN:] = acc_v[:SPAN - REST].astype(jnp.bfloat16)
    back_v_ref[...] = acc_v[SPAN - REST:SPAN].astype(jnp.bfloat16)
    dk_ref[...] = (scaling * acc_k[SPAN:2 * SPAN]).astype(jnp.bfloat16)
    dv_ref[...] = acc_v[SPAN:2 * SPAN].astype(jnp.bfloat16)
    dkx_ref[...] = scaling * acc_k[2 * SPAN:]
    dvx_ref[...] = acc_v[2 * SPAN:]
    token_ref[...] = jnp.zeros_like(token_ref)


def local_head(head, gates, prev_ok, q, k, v, g, halo, carry, after):
    rows, width = q.shape
    col = pl.BlockSpec((rows, HD), lambda i: (0, head))
    col_half = pl.BlockSpec((SPAN, HD), lambda i: (0, head))
    shapes = [
        jax.ShapeDtypeStruct((rows, width), jnp.float32),
        jax.ShapeDtypeStruct((rows, width), jnp.float32),
        jax.ShapeDtypeStruct((rows, width), jnp.bfloat16),
        jax.ShapeDtypeStruct((rows, width), jnp.bfloat16),
        jax.ShapeDtypeStruct((SPAN, width), jnp.float32),
        jax.ShapeDtypeStruct((SPAN, width), jnp.float32),
        jax.ShapeDtypeStruct((2 * SPAN - REST, width), jnp.bfloat16),
        jax.ShapeDtypeStruct((REST, width), jnp.bfloat16),
        jax.ShapeDtypeStruct((8, 128), jnp.float32),
    ]
    extra = list(carry) + list(after)
    result = pl.pallas_call(
        functools.partial(local_kernel, head, len(extra)),
        grid=(1,),
        out_shape=shapes,
        in_specs=[SMEM, SMEM, col, col, col, col, col] + [ANY] * len(extra),
        out_specs=[col, col, col_half, col_half, col_half, col_half,
                   pl.BlockSpec((2 * SPAN - REST, HD), lambda i: (0, head)),
                   pl.BlockSpec((REST, HD), lambda i: (0, head)),
                   pl.BlockSpec((8, 128), lambda i: (0, 0))],
        scratch_shapes=[
            pltpu.VMEM((3 * SPAN, HD), jnp.bfloat16),
            pltpu.VMEM((3 * SPAN, HD), jnp.bfloat16),
            pltpu.VMEM((HD, 3 * SPAN), jnp.bfloat16),
            pltpu.VMEM((HD, 3 * SPAN), jnp.bfloat16),
            pltpu.VMEM((3 * SPAN, HD), jnp.float32),
            pltpu.VMEM((3 * SPAN, HD), jnp.float32),
        ],
        input_output_aliases={7 + i: i for i in range(len(carry))},
        compiler_params=pltpu.CompilerParams(vmem_limit_bytes=VMEM_LIMIT),
        cost_estimate=pl.CostEstimate(flops=9 * 10**9, bytes_accessed=4 * 2**20,
                                      transcendentals=2 * 512 * 896),
        name="local_head",
    )(gates, prev_ok, q, k, v, g, halo, *extra)
    return result[:8], result[8]


def memory_kernel(n_src, n_any, call, bounds, loc, gates, q_ref, g_ref, lo_ref, dqf_ref, *rest):
    sources = rest[:n_src]
    out_ref, dq_ref, token_ref, buf, sems = rest[n_src + n_any:]
    token_ref[...] = jnp.zeros_like(token_ref)
    head = pl.program_id(0)
    start, stop = bounds[call], bounds[call + 1]
    scaling = HD ** -0.5

    def fetch(h, slot):
        for j in range(2 * R):
            code = loc[j // R, h, j % R]
            kind, index = code // KIND, lax.rem(code, KIND)

            def pick(low, high):
                if high - low == 1:
                    pltpu.make_async_copy(
                        sources[low].at[index], buf.at[slot, j], sems.at[slot, j]
                    ).start()
                    return
                middle = (low + high) // 2

                @pl.when(kind < middle)
                def _():
                    pick(low, middle)

                @pl.when(kind >= middle)
                def _():
                    pick(middle, high)

            pick(0, n_src)

    @pl.when((head == 0) & (start < stop))
    def _():
        fetch(start, lax.rem(start, 2))

    @pl.when((head >= start) & (head < stop))
    def _():
        slot = lax.rem(head, 2)

        @pl.when(head + 1 < stop)
        def _():
            fetch(head + 1, 1 - slot)

        for j in range(2 * R):
            pltpu.make_async_copy(sources[0].at[0], buf.at[slot, j], sems.at[slot, j]).wait()
        gate = gates[head]
        for span in range(2):
            blocks = buf[slot, pl.ds(span * R, R)]
            mk = blocks[:, :, :HD].reshape(R * BLOCK, HD)
            mv = blocks[:, :, HD:].reshape(R * BLOCK, HD)
            rows = pl.ds(span * SPAN, SPAN)
            q = q_ref[rows, :]
            gm = (gate * g_ref[rows, :].astype(jnp.float32)).astype(jnp.bfloat16)
            s = mm(q, mk, ((1,), (1,)))
            top = jnp.max(s, axis=1, keepdims=True)
            e = jnp.exp2((s - top) * (scaling * LOG2E))
            share = 1.0 / jnp.sum(e, axis=1, keepdims=True)
            mo = mm(e.astype(jnp.bfloat16), mv, ((1,), (0,))) * share
            dp = mm(gm, mv, ((1,), (1,)))
            dot = jnp.sum(gm.astype(jnp.float32) * mo, axis=1, keepdims=True)
            ds = (e * (dp - dot)).astype(jnp.bfloat16)
            dqm = mm(ds, mk, ((1,), (0,))) * (share * scaling)
            out_ref[rows, :] = (gate * mo + lo_ref[rows, :]).astype(jnp.bfloat16)
            dq_ref[rows, :] = (dqm + dqf_ref[rows, :]).astype(jnp.bfloat16)


def memory_heads(call, bounds, loc, gates, q, g, carry, sources, made, after=()):
    rows, width = q.shape
    heads = width // HD

    def column(h, bounds):
        start, stop = bounds[call], bounds[call + 1]
        return 0, jnp.clip(h, start, jnp.maximum(stop - 1, start))

    col = pl.BlockSpec((rows, HD), column)
    full = jax.ShapeDtypeStruct((rows, width), jnp.bfloat16)
    extra = list(made) + list(after)
    return pl.pallas_call(
        functools.partial(memory_kernel, len(sources), len(extra), call),
        grid_spec=pltpu.PrefetchScalarGridSpec(
            num_scalar_prefetch=1,
            grid=(heads,),
            in_specs=[SMEM, SMEM, col, col, col, col] + [ANY] * (len(sources) + len(extra)),
            out_specs=[col, col, pl.BlockSpec((16, 128), lambda h, bounds: (0, 0))],
            scratch_shapes=[
                pltpu.VMEM((2, 2 * R, BLOCK, 2 * HD), jnp.bfloat16),
                pltpu.SemaphoreType.DMA((2, 2 * R)),
            ],
        ),
        out_shape=[full, full, jax.ShapeDtypeStruct((16, 128), jnp.bfloat16)],
        input_output_aliases={7 + len(sources) + i: i for i in range(len(made))},
        compiler_params=pltpu.CompilerParams(vmem_limit_bytes=VMEM_LIMIT),
        cost_estimate=pl.CostEstimate(flops=14 * 10**9, bytes_accessed=2**20,
                                      transcendentals=heads * 2 * 512 * 512),
        name="memory_heads",
    )(bounds, loc, gates, q, g, carry[0], carry[1], *sources, *extra)


def close_kernel(dkx_ref, dvx_ref, bk_ref, bv_ref, dk_in, dv_in, after_ref, dk_ref, dv_ref):
    dk_ref[...] = (dkx_ref[...] + bk_ref[:SPAN].astype(jnp.float32)).astype(jnp.bfloat16)
    dv_ref[:SPAN - REST] = (
        dvx_ref[:SPAN - REST] + bk_ref[SPAN:].astype(jnp.float32)
    ).astype(jnp.bfloat16)
    dv_ref[SPAN - REST:] = (
        dvx_ref[SPAN - REST:] + bv_ref[...].astype(jnp.float32)
    ).astype(jnp.bfloat16)


def close_grads(carry, back_k, back_v, after):
    dk, dv, dkx, dvx = carry[2:6]
    width = dk.shape[1]
    part = width // 4
    upper = pl.BlockSpec((SPAN, part), lambda h: (0, h))
    lower = pl.BlockSpec((SPAN, part), lambda h: (1, h))
    return pl.pallas_call(
        close_kernel,
        grid=(4,),
        out_shape=[jax.ShapeDtypeStruct(dk.shape, dk.dtype)] * 2,
        in_specs=[upper, upper,
                  pl.BlockSpec((2 * SPAN - REST, part), lambda h: (0, h)),
                  pl.BlockSpec((REST, part), lambda h: (0, h))] + [ANY] * 3,
        out_specs=[lower, lower],
        input_output_aliases={4: 0, 5: 1},
        compiler_params=pltpu.CompilerParams(vmem_limit_bytes=VMEM_LIMIT),
        name="close_grads",
    )(dkx, dvx, back_k, back_v, dk, dv, after)


def exchange_all(memory, block_ids):
    tok_count = lax.axis_size("tok")
    heads_here, blocks_here = memory.shape[:2]
    wanted = block_ids.reshape(-1)
    request_count = wanted.shape[0]
    owner_rank = wanted // blocks_here
    head_index = jnp.arange(request_count) // R % heads_here
    request_code = head_index * blocks_here + wanted % blocks_here
    order_ids = jnp.arange(request_count)
    same_owner = owner_rank[:, None] == owner_rank[None, :]
    slot_index = jnp.sum(same_owner & (order_ids[None, :] < order_ids[:, None]), axis=1)
    capacity = 2 * request_count // tok_count
    to_owner = (owner_rank[:, None] == jnp.arange(tok_count)[None, :]).astype(jnp.int32)
    to_slot = (slot_index[:, None] == jnp.arange(capacity)[None, :]).astype(jnp.int32)
    request_table = jnp.sum(
        request_code[:, None, None] * to_owner[:, :, None] * to_slot[:, None, :], axis=0
    )
    mem_flat = memory.reshape(-1, BLOCK, memory.shape[-1])
    found = mem_flat[lax.all_to_all(request_table, "tok", split_axis=0, concat_axis=0, tiled=True)]
    returned = lax.all_to_all(found, "tok", split_axis=0, concat_axis=0, tiled=True)
    loc = (owner_rank * capacity + slot_index).reshape(block_ids.shape)
    return returned.reshape(-1, BLOCK, memory.shape[-1]), loc.astype(jnp.int32)


def pack_kernel(groups, n_src, n_any, table, *rest):
    sources = rest[:n_src]
    outs = rest[n_src + n_any:n_src + n_any + len(groups)]
    held, sems, sent = rest[-3:]
    sizes = [sum(count for row, count in group) for group in groups]
    for phase in range(2):
        number = 0
        for place, group in enumerate(groups):
            for row, count in group:
                for j in range(count):
                    code = table[row, j]
                    for kind, source in enumerate(sources):
                        @pl.when((code >= kind * KIND) & (code < (kind + 1) * KIND))
                        def _():
                            copy = pltpu.make_async_copy(
                                source.at[code - kind * KIND], held.at[number], sems.at[number]
                            )
                            copy.wait() if phase else copy.start()
                    number += 1
            if phase:
                pltpu.make_async_copy(
                    held.at[pl.ds(number - sizes[place], sizes[place])], outs[place],
                    sent.at[place],
                ).start()
    number = 0
    for place, size in enumerate(sizes):
        pltpu.make_async_copy(held.at[pl.ds(number, size)], outs[place], sent.at[place]).wait()
        number += size


def pack(table, sources, groups, after):
    sizes = [sum(count for row, count in group) for group in groups]
    block = sources[0].shape[1:]
    kind = sources[0].dtype
    return pl.pallas_call(
        functools.partial(pack_kernel, groups, len(sources), len(after)),
        out_shape=[jax.ShapeDtypeStruct((size,) + block, kind) for size in sizes],
        in_specs=[SMEM] + [ANY] * (len(sources) + len(after)),
        out_specs=[ANY] * len(groups),
        scratch_shapes=[
            pltpu.VMEM((sum(sizes),) + block, kind),
            pltpu.SemaphoreType.DMA((sum(sizes),)),
            pltpu.SemaphoreType.DMA((len(groups),)),
        ],
        compiler_params=pltpu.CompilerParams(vmem_limit_bytes=VMEM_LIMIT),
        cost_estimate=pl.CostEstimate(flops=0, bytes_accessed=2**16, transcendentals=0),
        name="pack",
    )(table, *sources, *after)


def held_back(x, after):
    def kernel(*refs):
        pass

    return pl.pallas_call(
        kernel,
        out_shape=jax.ShapeDtypeStruct(x.shape, x.dtype),
        in_specs=[ANY] * (1 + len(after)),
        out_specs=ANY,
        input_output_aliases={0: 0},
        cost_estimate=pl.CostEstimate(flops=0, bytes_accessed=0, transcendentals=0),
        name="held_back",
    )(x, *after)


def summed(parts, after):
    def kernel(*refs):
        total = refs[0][...]
        for ref in refs[1:len(parts)]:
            total = total + ref[...]
        refs[-1][...] = total

    x = parts[0]
    whole = pl.BlockSpec(memory_space=pltpu.VMEM)
    return pl.pallas_call(
        kernel,
        out_shape=jax.ShapeDtypeStruct(x.shape, x.dtype),
        in_specs=[whole] * len(parts) + [ANY] * len(after),
        out_specs=whole,
        compiler_params=pltpu.CompilerParams(vmem_limit_bytes=VMEM_LIMIT),
        cost_estimate=pl.CostEstimate(flops=0, bytes_accessed=2**16, transcendentals=0),
        name="summed",
    )(*parts, *after)


def tails(keys, values):
    width = keys.shape[1]
    block = pl.BlockSpec((SPAN, width), lambda i: (keys.shape[0] // SPAN - 1, 0))

    def kernel(k_ref, v_ref, out_ref):
        out_ref[:SPAN] = k_ref[...]
        out_ref[SPAN:] = v_ref[...]

    return pl.pallas_call(
        kernel,
        grid=(1,),
        out_shape=jax.ShapeDtypeStruct((2 * SPAN, width), keys.dtype),
        in_specs=[block, block],
        out_specs=pl.BlockSpec((2 * SPAN, width), lambda i: (0, 0)),
        compiler_params=pltpu.CompilerParams(vmem_limit_bytes=VMEM_LIMIT),
        name="tails",
    )(keys, values)


def plan(block_ids, everyone, heads, blocks_here):
    tok_count = lax.axis_size("tok")
    chips = tok_count // 2
    shard = heads * blocks_here
    here = lax.axis_index("tok")
    chip, core = here // 2, here % 2
    head_of = jnp.arange(heads, dtype=jnp.int32)[None, :, None]
    block = (everyone // blocks_here) * shard + head_of * blocks_here + everyone % blocks_here
    universe = jnp.arange(tok_count * shard, dtype=jnp.int32)
    each = jnp.any(block.reshape(tok_count, -1)[:, :, None] == universe, axis=1)
    need = each.reshape(chips, 2, -1).any(axis=1).reshape(chips, tok_count, shard)
    sibling = lax.dynamic_slice(each, (here ^ 1, here * shard), (1, shard))
    before = jnp.triu(jnp.ones((shard, shard), jnp.bfloat16), 1)

    def ranked(wanted):
        rank = jnp.dot(wanted.astype(jnp.bfloat16), before, preferred_element_type=jnp.float32)
        return jnp.where(wanted, rank.astype(jnp.int32), -1)

    rank = ranked(need)
    count = jnp.sum(need.astype(jnp.int32), axis=2)
    partner = count.reshape(chips, chips, 2)[:, :, ::-1].reshape(count.shape)
    left = jnp.maximum(count - MAIN, 0)
    given = jnp.minimum(jnp.minimum(left, jnp.maximum(MAIN - partner, 0)), HANDED)
    rest = (left - given).reshape(chips, chips, 2)
    ahead = jnp.stack([jnp.zeros_like(rest[..., 0]), rest[..., 0]], axis=2).reshape(count.shape)
    most = jnp.max(jnp.where(jnp.eye(chips, dtype=bool), 0, rest.sum(axis=2)), axis=0)
    core_of = jnp.arange(tok_count, dtype=jnp.int32)[:, None] % 2
    over = rank - MAIN
    is_given = (over >= 0) & (over < given[:, :, None])
    is_second = over >= given[:, :, None]
    turn = over - given[:, :, None] + ahead[:, :, None]
    lane = jnp.where(is_second, turn % 2, jnp.where(is_given, 1 - core_of, core_of))
    spot = jnp.where(is_second, turn // 2, jnp.where(is_given, partner[:, :, None] + over, rank))

    chip_ids = jnp.arange(chips, dtype=jnp.int32)[:, None]
    index = jnp.arange(1, shard + 1, dtype=jnp.int32)

    def of_device(device):
        def cut(x):
            return lax.dynamic_index_in_dim(x, device, 1, keepdims=False)
        live = (cut(rank) >= 0) & (chip_ids != chip)
        return live, cut(is_given), cut(is_second), cut(lane), cut(spot), cut(over)

    def listed(live, spots, size, names):
        slots = jnp.arange(size, dtype=jnp.int32)[None, :, None]
        hit = live[:, None, :] & (spots[:, None, :] == slots)
        return jnp.sum(jnp.where(hit, names[:, None, :], 0), axis=2)

    live, my_given, my_second, my_lane, my_spot, my_over = of_device(here)
    names = jnp.broadcast_to(index, live.shape)
    side = listed(live & my_given, my_over, MAIN, names) - 1
    side_second = listed(live & my_second & (my_lane != core), my_spot, MAIN, names) - 1
    main = listed(live & ~my_second & ~my_given, my_spot, MAIN, names)
    second = listed(live & my_second & (my_lane == core), my_spot, MAIN, names)
    live, sib_given, sib_second, sib_lane, sib_spot, sib_over = of_device(here ^ 1)
    main += listed(live & sib_given, sib_spot, MAIN, KIND + 1 + HANDED * chip_ids + sib_over)
    second += listed(
        live & sib_second & (sib_lane == core), sib_spot, MAIN,
        KIND + 1 + SECOND * chip_ids + sib_spot,
    )
    beside = listed(ranked(sibling) >= 0, ranked(sibling), MAIN, index[None, :])
    main = jnp.where(chip_ids == chip, beside, main) - 1
    table = jnp.concatenate([side, main, side_second, second - 1])
    sender = jnp.arange(tok_count, dtype=jnp.int32)[:, None]
    to_me = [lax.dynamic_index_in_dim(x, chip, 0, keepdims=False) for x in (is_second, lane, spot)]
    away = (to_me[1] != core).astype(jnp.int32)
    place = jnp.where(
        to_me[0], (3 + away) * KIND + to_me[2],
        (1 + away) * KIND + MAIN * (sender // 2) + to_me[2],
    )
    mine = ranked(lax.dynamic_slice(each, (here, (here ^ 1) * shard), (1, shard)))
    place = jnp.where(sender == here, jnp.arange(shard, dtype=jnp.int32), place)
    place = jnp.where(sender == here ^ 1, 2 * KIND + MAIN * chip + mine, place).reshape(-1)
    own = (block_ids // blocks_here) * shard + head_of * blocks_here + block_ids % blocks_here
    loc = jnp.sum(jnp.where(own.reshape(-1, 1) == universe, place, 0), axis=1)
    loc = loc.reshape(block_ids.shape)
    waits = jnp.any(loc >= 3 * KIND, axis=(0, 2))
    ready = jnp.min(jnp.where(waits, jnp.arange(heads), heads - 1))
    return table, loc, most, jnp.stack([jnp.int32(0), ready.astype(jnp.int32), jnp.int32(heads)])


def between_chips(block):
    count = lax.axis_size("tok")
    groups = [[i for i in range(count) if i % 2 == core] for core in range(2)]
    return lax.all_to_all(
        block, "tok", split_axis=0, concat_axis=0, axis_index_groups=groups, tiled=True
    )


def chip_shift(block, source, distance):
    count = lax.axis_size("tok")
    route = [(i, (i + 2 * distance) % count) for i in (2 * source, 2 * source + 1)]
    return lax.ppermute(block, "tok", route)


def core_swap(block):
    return lax.ppermute(block, "tok", [(i, i ^ 1) for i in range(lax.axis_size("tok"))])


def most_of_all(most):
    count = lax.axis_size("mem")
    step = 1
    while step < count:
        other = lax.ppermute(most, "mem", [(i, i ^ step) for i in range(count)])
        most = jnp.maximum(most, other)
        step *= 2
    return most


def per_device(queries, keys, values, memory, block_ids, gate_bias, grad_out):
    my_rank = lax.axis_index("tok")
    tok_count = lax.axis_size("tok")
    heads, blocks_here = memory.shape[:2]
    chips = tok_count // 2
    direct = chips == 4 and lax.axis_size("mem") == 4
    gates = jax.nn.sigmoid(gate_bias)
    prev_ok = (my_rank > 0).astype(jnp.int32).reshape(1)
    if direct:
        everyone = lax.all_to_all(
            jnp.broadcast_to(block_ids[None], (tok_count,) + block_ids.shape),
            "tok", split_axis=0, concat_axis=0, tiled=True,
        )
    tail = tails(keys, values)
    halo = passed_along(tail, "tok", 1)
    carry, token = (), ()
    if direct:
        near = memory.reshape(-1, BLOCK, memory.shape[-1])
        table, loc, most, bounds = plan(block_ids, everyone, heads, blocks_here)
        (side,) = pack(
            table, [near], [[(chip, HANDED) for chip in range(chips)]], (tail,)
        )
        handed = core_swap(side)
        (main,) = pack(
            table, [near, handed], [[(chips + chip, MAIN) for chip in range(chips)]], ()
        )
        own_main = between_chips(main)
        (side,) = pack(
            table, [near], [[(2 * chips + chip, SECOND) for chip in range(chips)]], (main,)
        )
        handed = core_swap(side)
        token = (side,)
    for head in range(heads):
        if direct and head == 4:
            token = token + (loc, bounds, most)
        carry, token = local_head(
            head, gates, prev_ok, queries, keys, values, grad_out, halo, carry, token
        )
        if direct and head == 1:
            most = jnp.broadcast_to(jnp.pad(most, (0, 8 - chips))[:, None], (8, 128))
            most = most_of_all(most + token.astype(jnp.int32))
            hot = jnp.argmax(most[:chips, 0]).astype(jnp.int32)
            limit = jnp.where(jnp.arange(chips) == hot, 2 * SECOND, 0)
            overflow = jnp.any(most[:chips, 0] > limit)
            branch = jnp.where(overflow, chips, hot)
        token = (token,)

    def finish(start, stop, where, sources, made):
        return memory_heads(
            start, stop, where, gates, queries, grad_out, carry, sources, made
        )

    def full_exchange(halo_grad):
        returned, where = exchange_all(memory, block_ids)
        out, dq, _ = finish(0, jnp.array([0, heads], jnp.int32), where, [returned], ())
        return out, dq, passed_along(halo_grad, "tok", -1)

    back_k = passed_along(carry[6], "tok", -1)
    if not direct:
        out, dq, back_v = full_exchange(carry[7])
        return out, dq, *close_grads(carry, back_k, back_v, block_ids)

    def from_chip(source):
        def send(halo_grad):
            late = [chip_shift(seconds[(source + k) % chips], source, k) for k in range(1, chips)]
            back = passed_along(halo_grad, "tok", -1)
            sources = [near, own_main, core_swap(own_main)]
            *made, made_token = finish(0, bounds, loc, sources, ())
            late = summed(late, (made_token,))
            sources += [late, core_swap(late)]
            out, dq, _ = finish(1, bounds, loc, sources, made)
            return out, dq, back
        return send

    seconds = pack(
        table, [near, handed], [[(3 * chips + chip, SECOND)] for chip in range(chips)], token
    )
    own_main = held_back(own_main, seconds)
    out, dq, back_v = lax.switch(
        branch, [from_chip(source) for source in range(chips)] + [full_exchange], carry[7]
    )
    dk, dv = close_grads(carry, back_k, back_v, out)
    return out, dq, dk, dv


def solution(mesh):
    in_specs = (
        P("tok", "mem"),
        P("tok", "mem"),
        P("tok", "mem"),
        P("mem", "tok", None, None),
        P("tok", "mem", None),
        P("mem"),
        P("tok", "mem"),
    )
    out_specs = (P("tok", "mem"), P("tok", "mem"), P("tok", "mem"), P("tok", "mem"))
    return jax.shard_map(
        per_device, mesh=mesh, in_specs=in_specs, out_specs=out_specs, check_vma=False
    )
```

```python
import functools

import jax
import jax.numpy as jnp
from jax import lax
from jax.experimental import pallas as pl
from jax.experimental.pallas import tpu as pltpu
from jax.sharding import PartitionSpec as P

SPAN = 512
HALF = 256
BLOCK = 128
R = 4
HD = 128
NEG = -1e30
LOG2E = 1.4426950408889634
KIND = 512
VMEM_LIMIT = 56 * 2**20
MAIN = 19
HANDED = 5
SECOND = 6
REST = 256
ANY = pl.BlockSpec(memory_space=pl.ANY)
SMEM = pl.BlockSpec(memory_space=pltpu.SMEM)


def passed_along(block, axis, distance):
    devices = range(lax.axis_size(axis))
    route = [(i - distance, i) for i in devices if i - distance in devices]
    return lax.ppermute(block, axis, route)


def mm(a, b, dims):
    return lax.dot_general(a, b, (dims, ((), ())), preferred_element_type=jnp.float32)


def local_kernel(head, n_any, gates, prev_ok, q_ref, k_ref, v_ref, g_ref, halo_ref, *rest):
    (lo_ref, dq_ref, dk_ref, dv_ref, dkx_ref, dvx_ref, back_k_ref, back_v_ref, token_ref,
     kx, vx, kt, vt, acc_k, acc_v) = rest[n_any:]
    scaling = HD ** -0.5
    keep = 1.0 - gates[head]
    kx[:SPAN] = halo_ref[:SPAN]
    kx[SPAN:] = k_ref[...]
    vx[:SPAN] = halo_ref[SPAN:]
    vx[SPAN:] = v_ref[...]
    kt[...] = kx[...].T
    vt[...] = vx[...].T
    ok = prev_ok[0] > 0
    tri = (lax.broadcasted_iota(jnp.int32, (HALF, HALF), 0)
           <= lax.broadcasted_iota(jnp.int32, (HALF, HALF), 1))
    for span in range(2):
        for half in range(2):
            row0 = span * SPAN + half * HALF
            win0 = span * SPAN
            width = SPAN + HALF * (half + 1)
            rows = pl.ds(row0, HALF)
            win = pl.ds(win0, width)
            q = q_ref[rows, :]
            gl = (keep * g_ref[rows, :].astype(jnp.float32)).astype(jnp.bfloat16)
            st = mm(kx[win, :], q, ((1,), (1,))) * scaling
            first = st[:SPAN]
            if span == 0:
                first = jnp.where(ok, first, NEG)
            parts = [first]
            if half:
                parts.append(st[SPAN:width - HALF])
            parts.append(jnp.where(tri, st[width - HALF:], NEG))
            st = jnp.concatenate(parts, axis=0)
            top = jnp.max(st, axis=0, keepdims=True)
            e = jnp.exp(st - top)
            total = jnp.sum(e, axis=0, keepdims=True)
            pt = (e * (1.0 / total)).astype(jnp.bfloat16)
            out_t = mm(vt[:, win], pt, ((1,), (0,)))
            gt = gl.astype(jnp.float32).T
            dot = jnp.sum(gt * out_t, axis=0, keepdims=True)
            dpt = mm(vx[win, :], gl, ((1,), (1,)))
            dst = (pt.astype(jnp.float32) * (dpt - dot)).astype(jnp.bfloat16)
            dq_t = mm(kt[:, win], dst, ((1,), (0,)))
            lo_ref[rows, :] = keep * out_t.T
            dq_ref[rows, :] = scaling * dq_t.T
            dkw = mm(dst, q, ((1,), (0,)))
            dvw = mm(pt, gl, ((1,), (0,)))
            if span == 0 and half == 0:
                acc_k[win, :] = dkw
                acc_v[win, :] = dvw
            else:
                old = 768 if span == 0 else (1024 if half == 0 else 1280)
                seen = max(0, min(old, win0 + width) - win0)
                acc_k[pl.ds(win0, seen), :] += dkw[:seen]
                acc_v[pl.ds(win0, seen), :] += dvw[:seen]
                if seen < width:
                    acc_k[pl.ds(win0 + seen, width - seen), :] = dkw[seen:]
                    acc_v[pl.ds(win0 + seen, width - seen), :] = dvw[seen:]
    back_k_ref[:SPAN] = (scaling * acc_k[:SPAN]).astype(jnp.bfloat16)
    back_k_ref[SPAN:] = acc_v[:SPAN - REST].astype(jnp.bfloat16)
    back_v_ref[...] = acc_v[SPAN - REST:SPAN].astype(jnp.bfloat16)
    dk_ref[...] = (scaling * acc_k[SPAN:2 * SPAN]).astype(jnp.bfloat16)
    dv_ref[...] = acc_v[SPAN:2 * SPAN].astype(jnp.bfloat16)
    dkx_ref[...] = scaling * acc_k[2 * SPAN:]
    dvx_ref[...] = acc_v[2 * SPAN:]
    token_ref[...] = jnp.zeros_like(token_ref)


def local_head(head, gates, prev_ok, q, k, v, g, halo, carry, after):
    rows, width = q.shape
    col = pl.BlockSpec((rows, HD), lambda i: (0, head))
    col_half = pl.BlockSpec((SPAN, HD), lambda i: (0, head))
    shapes = [
        jax.ShapeDtypeStruct((rows, width), jnp.float32),
        jax.ShapeDtypeStruct((rows, width), jnp.float32),
        jax.ShapeDtypeStruct((rows, width), jnp.bfloat16),
        jax.ShapeDtypeStruct((rows, width), jnp.bfloat16),
        jax.ShapeDtypeStruct((SPAN, width), jnp.float32),
        jax.ShapeDtypeStruct((SPAN, width), jnp.float32),
        jax.ShapeDtypeStruct((2 * SPAN - REST, width), jnp.bfloat16),
        jax.ShapeDtypeStruct((REST, width), jnp.bfloat16),
        jax.ShapeDtypeStruct((8, 128), jnp.float32),
    ]
    extra = list(carry) + list(after)
    result = pl.pallas_call(
        functools.partial(local_kernel, head, len(extra)),
        grid=(1,),
        out_shape=shapes,
        in_specs=[SMEM, SMEM, col, col, col, col, col] + [ANY] * len(extra),
        out_specs=[col, col, col_half, col_half, col_half, col_half,
                   pl.BlockSpec((2 * SPAN - REST, HD), lambda i: (0, head)),
                   pl.BlockSpec((REST, HD), lambda i: (0, head)),
                   pl.BlockSpec((8, 128), lambda i: (0, 0))],
        scratch_shapes=[
            pltpu.VMEM((3 * SPAN, HD), jnp.bfloat16),
            pltpu.VMEM((3 * SPAN, HD), jnp.bfloat16),
            pltpu.VMEM((HD, 3 * SPAN), jnp.bfloat16),
            pltpu.VMEM((HD, 3 * SPAN), jnp.bfloat16),
            pltpu.VMEM((3 * SPAN, HD), jnp.float32),
            pltpu.VMEM((3 * SPAN, HD), jnp.float32),
        ],
        input_output_aliases={7 + i: i for i in range(len(carry))},
        compiler_params=pltpu.CompilerParams(vmem_limit_bytes=VMEM_LIMIT),
        cost_estimate=pl.CostEstimate(flops=9 * 10**9, bytes_accessed=4 * 2**20,
                                      transcendentals=2 * 512 * 896),
        name="local_head",
    )(gates, prev_ok, q, k, v, g, halo, *extra)
    return result[:8], result[8]


def memory_kernel(n_src, n_any, call, bounds, loc, gates, q_ref, g_ref, lo_ref, dqf_ref, *rest):
    sources = rest[:n_src]
    out_ref, dq_ref, token_ref, buf, sems = rest[n_src + n_any:]
    token_ref[...] = jnp.zeros_like(token_ref)
    head = pl.program_id(0)
    start, stop = bounds[call], bounds[call + 1]
    scaling = HD ** -0.5

    def fetch(h, slot):
        for j in range(2 * R):
            code = loc[j // R, h, j % R]
            kind, index = code // KIND, lax.rem(code, KIND)

            def pick(low, high):
                if high - low == 1:
                    pltpu.make_async_copy(
                        sources[low].at[index], buf.at[slot, j], sems.at[slot, j]
                    ).start()
                    return
                middle = (low + high) // 2

                @pl.when(kind < middle)
                def _():
                    pick(low, middle)

                @pl.when(kind >= middle)
                def _():
                    pick(middle, high)

            pick(0, n_src)

    @pl.when((head == 0) & (start < stop))
    def _():
        fetch(start, lax.rem(start, 2))

    @pl.when((head >= start) & (head < stop))
    def _():
        slot = lax.rem(head, 2)

        @pl.when(head + 1 < stop)
        def _():
            fetch(head + 1, 1 - slot)

        for j in range(2 * R):
            pltpu.make_async_copy(sources[0].at[0], buf.at[slot, j], sems.at[slot, j]).wait()
        gate = gates[head]
        for span in range(2):
            blocks = buf[slot, pl.ds(span * R, R)]
            mk = blocks[:, :, :HD].reshape(R * BLOCK, HD)
            mv = blocks[:, :, HD:].reshape(R * BLOCK, HD)
            rows = pl.ds(span * SPAN, SPAN)
            q = q_ref[rows, :]
            gm = (gate * g_ref[rows, :].astype(jnp.float32)).astype(jnp.bfloat16)
            s = mm(q, mk, ((1,), (1,)))
            top = jnp.max(s, axis=1, keepdims=True)
            e = jnp.exp2((s - top) * (scaling * LOG2E))
            share = 1.0 / jnp.sum(e, axis=1, keepdims=True)
            mo = mm(e.astype(jnp.bfloat16), mv, ((1,), (0,))) * share
            dp = mm(gm, mv, ((1,), (1,)))
            dot = jnp.sum(gm.astype(jnp.float32) * mo, axis=1, keepdims=True)
            ds = (e * (dp - dot)).astype(jnp.bfloat16)
            dqm = mm(ds, mk, ((1,), (0,))) * (share * scaling)
            out_ref[rows, :] = (gate * mo + lo_ref[rows, :]).astype(jnp.bfloat16)
            dq_ref[rows, :] = (dqm + dqf_ref[rows, :]).astype(jnp.bfloat16)


def memory_heads(call, bounds, loc, gates, q, g, carry, sources, made, after=()):
    rows, width = q.shape
    heads = width // HD

    def column(h, bounds):
        start, stop = bounds[call], bounds[call + 1]
        return 0, jnp.clip(h, start, jnp.maximum(stop - 1, start))

    col = pl.BlockSpec((rows, HD), column)
    full = jax.ShapeDtypeStruct((rows, width), jnp.bfloat16)
    extra = list(made) + list(after)
    return pl.pallas_call(
        functools.partial(memory_kernel, len(sources), len(extra), call),
        grid_spec=pltpu.PrefetchScalarGridSpec(
            num_scalar_prefetch=1,
            grid=(heads,),
            in_specs=[SMEM, SMEM, col, col, col, col] + [ANY] * (len(sources) + len(extra)),
            out_specs=[col, col, pl.BlockSpec((16, 128), lambda h, bounds: (0, 0))],
            scratch_shapes=[
                pltpu.VMEM((2, 2 * R, BLOCK, 2 * HD), jnp.bfloat16),
                pltpu.SemaphoreType.DMA((2, 2 * R)),
            ],
        ),
        out_shape=[full, full, jax.ShapeDtypeStruct((16, 128), jnp.bfloat16)],
        input_output_aliases={7 + len(sources) + i: i for i in range(len(made))},
        compiler_params=pltpu.CompilerParams(vmem_limit_bytes=VMEM_LIMIT),
        cost_estimate=pl.CostEstimate(flops=14 * 10**9, bytes_accessed=2**20,
                                      transcendentals=heads * 2 * 512 * 512),
        name="memory_heads",
    )(bounds, loc, gates, q, g, carry[0], carry[1], *sources, *extra)


def close_kernel(dkx_ref, dvx_ref, bk_ref, bv_ref, dk_in, dv_in, after_ref, dk_ref, dv_ref):
    dk_ref[...] = (dkx_ref[...] + bk_ref[:SPAN].astype(jnp.float32)).astype(jnp.bfloat16)
    dv_ref[:SPAN - REST] = (
        dvx_ref[:SPAN - REST] + bk_ref[SPAN:].astype(jnp.float32)
    ).astype(jnp.bfloat16)
    dv_ref[SPAN - REST:] = (
        dvx_ref[SPAN - REST:] + bv_ref[...].astype(jnp.float32)
    ).astype(jnp.bfloat16)


def close_grads(carry, back_k, back_v, after):
    dk, dv, dkx, dvx = carry[2:6]
    width = dk.shape[1]
    part = width // 2
    upper = pl.BlockSpec((SPAN, part), lambda h: (0, h))
    lower = pl.BlockSpec((SPAN, part), lambda h: (1, h))
    return pl.pallas_call(
        close_kernel,
        grid=(2,),
        out_shape=[jax.ShapeDtypeStruct(dk.shape, dk.dtype)] * 2,
        in_specs=[upper, upper,
                  pl.BlockSpec((2 * SPAN - REST, part), lambda h: (0, h)),
                  pl.BlockSpec((REST, part), lambda h: (0, h))] + [ANY] * 3,
        out_specs=[lower, lower],
        input_output_aliases={4: 0, 5: 1},
        compiler_params=pltpu.CompilerParams(vmem_limit_bytes=VMEM_LIMIT),
        name="close_grads",
    )(dkx, dvx, back_k, back_v, dk, dv, after)


def exchange_all(memory, block_ids):
    tok_count = lax.axis_size("tok")
    heads_here, blocks_here = memory.shape[:2]
    wanted = block_ids.reshape(-1)
    request_count = wanted.shape[0]
    owner_rank = wanted // blocks_here
    head_index = jnp.arange(request_count) // R % heads_here
    request_code = head_index * blocks_here + wanted % blocks_here
    order_ids = jnp.arange(request_count)
    same_owner = owner_rank[:, None] == owner_rank[None, :]
    slot_index = jnp.sum(same_owner & (order_ids[None, :] < order_ids[:, None]), axis=1)
    capacity = 2 * request_count // tok_count
    to_owner = (owner_rank[:, None] == jnp.arange(tok_count)[None, :]).astype(jnp.int32)
    to_slot = (slot_index[:, None] == jnp.arange(capacity)[None, :]).astype(jnp.int32)
    request_table = jnp.sum(
        request_code[:, None, None] * to_owner[:, :, None] * to_slot[:, None, :], axis=0
    )
    mem_flat = memory.reshape(-1, BLOCK, memory.shape[-1])
    found = mem_flat[lax.all_to_all(request_table, "tok", split_axis=0, concat_axis=0, tiled=True)]
    returned = lax.all_to_all(found, "tok", split_axis=0, concat_axis=0, tiled=True)
    loc = (owner_rank * capacity + slot_index).reshape(block_ids.shape)
    return returned.reshape(-1, BLOCK, memory.shape[-1]), loc.astype(jnp.int32)


def pack_kernel(groups, n_src, n_any, table, *rest):
    sources = rest[:n_src]
    outs = rest[n_src + n_any:n_src + n_any + len(groups)]
    held, sems, sent = rest[-3:]
    sizes = [sum(count for row, count in group) for group in groups]
    for phase in range(2):
        number = 0
        for place, group in enumerate(groups):
            for row, count in group:
                for j in range(count):
                    code = table[row, j]
                    for kind, source in enumerate(sources):
                        @pl.when((code >= kind * KIND) & (code < (kind + 1) * KIND))
                        def _():
                            copy = pltpu.make_async_copy(
                                source.at[code - kind * KIND], held.at[number], sems.at[number]
                            )
                            copy.wait() if phase else copy.start()
                    number += 1
            if phase:
                pltpu.make_async_copy(
                    held.at[pl.ds(number - sizes[place], sizes[place])], outs[place],
                    sent.at[place],
                ).start()
    number = 0
    for place, size in enumerate(sizes):
        pltpu.make_async_copy(held.at[pl.ds(number, size)], outs[place], sent.at[place]).wait()
        number += size


def pack(table, sources, groups, after):
    sizes = [sum(count for row, count in group) for group in groups]
    block = sources[0].shape[1:]
    kind = sources[0].dtype
    return pl.pallas_call(
        functools.partial(pack_kernel, groups, len(sources), len(after)),
        out_shape=[jax.ShapeDtypeStruct((size,) + block, kind) for size in sizes],
        in_specs=[SMEM] + [ANY] * (len(sources) + len(after)),
        out_specs=[ANY] * len(groups),
        scratch_shapes=[
            pltpu.VMEM((sum(sizes),) + block, kind),
            pltpu.SemaphoreType.DMA((sum(sizes),)),
            pltpu.SemaphoreType.DMA((len(groups),)),
        ],
        compiler_params=pltpu.CompilerParams(vmem_limit_bytes=VMEM_LIMIT),
        cost_estimate=pl.CostEstimate(flops=0, bytes_accessed=2**16, transcendentals=0),
        name="pack",
    )(table, *sources, *after)


def held_back(x, after):
    def kernel(*refs):
        pass

    return pl.pallas_call(
        kernel,
        out_shape=jax.ShapeDtypeStruct(x.shape, x.dtype),
        in_specs=[ANY] * (1 + len(after)),
        out_specs=ANY,
        input_output_aliases={0: 0},
        cost_estimate=pl.CostEstimate(flops=0, bytes_accessed=0, transcendentals=0),
        name="held_back",
    )(x, *after)


def summed(parts, after):
    def kernel(*refs):
        total = refs[0][...]
        for ref in refs[1:len(parts)]:
            total = total + ref[...]
        refs[-1][...] = total

    x = parts[0]
    whole = pl.BlockSpec(memory_space=pltpu.VMEM)
    return pl.pallas_call(
        kernel,
        out_shape=jax.ShapeDtypeStruct(x.shape, x.dtype),
        in_specs=[whole] * len(parts) + [ANY] * len(after),
        out_specs=whole,
        compiler_params=pltpu.CompilerParams(vmem_limit_bytes=VMEM_LIMIT),
        cost_estimate=pl.CostEstimate(flops=0, bytes_accessed=2**16, transcendentals=0),
        name="summed",
    )(*parts, *after)


def tails(keys, values):
    width = keys.shape[1]
    block = pl.BlockSpec((SPAN, width), lambda i: (keys.shape[0] // SPAN - 1, 0))

    def kernel(k_ref, v_ref, out_ref):
        out_ref[:SPAN] = k_ref[...]
        out_ref[SPAN:] = v_ref[...]

    return pl.pallas_call(
        kernel,
        grid=(1,),
        out_shape=jax.ShapeDtypeStruct((2 * SPAN, width), keys.dtype),
        in_specs=[block, block],
        out_specs=pl.BlockSpec((2 * SPAN, width), lambda i: (0, 0)),
        compiler_params=pltpu.CompilerParams(vmem_limit_bytes=VMEM_LIMIT),
        name="tails",
    )(keys, values)


def plan(block_ids, everyone, heads, blocks_here):
    tok_count = lax.axis_size("tok")
    chips = tok_count // 2
    shard = heads * blocks_here
    here = lax.axis_index("tok")
    chip, core = here // 2, here % 2
    head_of = jnp.arange(heads, dtype=jnp.int32)[None, :, None]
    block = (everyone // blocks_here) * shard + head_of * blocks_here + everyone % blocks_here
    universe = jnp.arange(tok_count * shard, dtype=jnp.int32)
    each = jnp.any(block.reshape(tok_count, -1)[:, :, None] == universe, axis=1)
    need = each.reshape(chips, 2, -1).any(axis=1).reshape(chips, tok_count, shard)
    sibling = lax.dynamic_slice(each, (here ^ 1, here * shard), (1, shard))
    before = jnp.triu(jnp.ones((shard, shard), jnp.bfloat16), 1)

    def ranked(wanted):
        rank = jnp.dot(wanted.astype(jnp.bfloat16), before, preferred_element_type=jnp.float32)
        return jnp.where(wanted, rank.astype(jnp.int32), -1)

    rank = ranked(need)
    count = jnp.sum(need.astype(jnp.int32), axis=2)
    partner = count.reshape(chips, chips, 2)[:, :, ::-1].reshape(count.shape)
    left = jnp.maximum(count - MAIN, 0)
    given = jnp.minimum(jnp.minimum(left, jnp.maximum(MAIN - partner, 0)), HANDED)
    rest = (left - given).reshape(chips, chips, 2)
    ahead = jnp.stack([jnp.zeros_like(rest[..., 0]), rest[..., 0]], axis=2).reshape(count.shape)
    most = jnp.max(jnp.where(jnp.eye(chips, dtype=bool), 0, rest.sum(axis=2)), axis=0)
    core_of = jnp.arange(tok_count, dtype=jnp.int32)[:, None] % 2
    over = rank - MAIN
    is_given = (over >= 0) & (over < given[:, :, None])
    is_second = over >= given[:, :, None]
    turn = over - given[:, :, None] + ahead[:, :, None]
    lane = jnp.where(is_second, turn % 2, jnp.where(is_given, 1 - core_of, core_of))
    spot = jnp.where(is_second, turn // 2, jnp.where(is_given, partner[:, :, None] + over, rank))

    chip_ids = jnp.arange(chips, dtype=jnp.int32)[:, None]
    index = jnp.arange(1, shard + 1, dtype=jnp.int32)

    def of_device(device):
        def cut(x):
            return lax.dynamic_index_in_dim(x, device, 1, keepdims=False)
        live = (cut(rank) >= 0) & (chip_ids != chip)
        return live, cut(is_given), cut(is_second), cut(lane), cut(spot), cut(over)

    def listed(live, spots, size, names):
        slots = jnp.arange(size, dtype=jnp.int32)[None, :, None]
        hit = live[:, None, :] & (spots[:, None, :] == slots)
        return jnp.sum(jnp.where(hit, names[:, None, :], 0), axis=2)

    live, my_given, my_second, my_lane, my_spot, my_over = of_device(here)
    names = jnp.broadcast_to(index, live.shape)
    side = listed(live & my_given, my_over, MAIN, names) - 1
    side_second = listed(live & my_second & (my_lane != core), my_spot, MAIN, names) - 1
    main = listed(live & ~my_second & ~my_given, my_spot, MAIN, names)
    second = listed(live & my_second & (my_lane == core), my_spot, MAIN, names)
    live, sib_given, sib_second, sib_lane, sib_spot, sib_over = of_device(here ^ 1)
    main += listed(live & sib_given, sib_spot, MAIN, KIND + 1 + HANDED * chip_ids + sib_over)
    second += listed(
        live & sib_second & (sib_lane == core), sib_spot, MAIN,
        KIND + 1 + SECOND * chip_ids + sib_spot,
    )
    beside = listed(ranked(sibling) >= 0, ranked(sibling), MAIN, index[None, :])
    main = jnp.where(chip_ids == chip, beside, main) - 1
    table = jnp.concatenate([side, main, side_second, second - 1])
    sender = jnp.arange(tok_count, dtype=jnp.int32)[:, None]
    to_me = [lax.dynamic_index_in_dim(x, chip, 0, keepdims=False) for x in (is_second, lane, spot)]
    away = (to_me[1] != core).astype(jnp.int32)
    place = jnp.where(
        to_me[0], (3 + away) * KIND + to_me[2],
        (1 + away) * KIND + MAIN * (sender // 2) + to_me[2],
    )
    mine = ranked(lax.dynamic_slice(each, (here, (here ^ 1) * shard), (1, shard)))
    place = jnp.where(sender == here, jnp.arange(shard, dtype=jnp.int32), place)
    place = jnp.where(sender == here ^ 1, 2 * KIND + MAIN * chip + mine, place).reshape(-1)
    own = (block_ids // blocks_here) * shard + head_of * blocks_here + block_ids % blocks_here
    loc = jnp.sum(jnp.where(own.reshape(-1, 1) == universe, place, 0), axis=1)
    loc = loc.reshape(block_ids.shape)
    waits = jnp.any(loc >= 3 * KIND, axis=(0, 2))
    ready = jnp.min(jnp.where(waits, jnp.arange(heads), heads - 1))
    return table, loc, most, jnp.stack([jnp.int32(0), ready.astype(jnp.int32), jnp.int32(heads)])


def between_chips(block):
    count = lax.axis_size("tok")
    groups = [[i for i in range(count) if i % 2 == core] for core in range(2)]
    return lax.all_to_all(
        block, "tok", split_axis=0, concat_axis=0, axis_index_groups=groups, tiled=True
    )


def chip_shift(block, source, distance):
    count = lax.axis_size("tok")
    route = [(i, (i + 2 * distance) % count) for i in (2 * source, 2 * source + 1)]
    return lax.ppermute(block, "tok", route)


def core_swap(block):
    return lax.ppermute(block, "tok", [(i, i ^ 1) for i in range(lax.axis_size("tok"))])


def most_of_all(most):
    count = lax.axis_size("mem")
    step = 1
    while step < count:
        other = lax.ppermute(most, "mem", [(i, i ^ step) for i in range(count)])
        most = jnp.maximum(most, other)
        step *= 2
    return most


def per_device(queries, keys, values, memory, block_ids, gate_bias, grad_out):
    my_rank = lax.axis_index("tok")
    tok_count = lax.axis_size("tok")
    heads, blocks_here = memory.shape[:2]
    chips = tok_count // 2
    direct = chips == 4 and lax.axis_size("mem") == 4
    gates = jax.nn.sigmoid(gate_bias)
    prev_ok = (my_rank > 0).astype(jnp.int32).reshape(1)
    if direct:
        everyone = lax.all_to_all(
            jnp.broadcast_to(block_ids[None], (tok_count,) + block_ids.shape),
            "tok", split_axis=0, concat_axis=0, tiled=True,
        )
    tail = tails(keys, values)
    halo = passed_along(tail, "tok", 1)
    carry, token = (), ()
    if direct:
        near = memory.reshape(-1, BLOCK, memory.shape[-1])
        table, loc, most, bounds = plan(block_ids, everyone, heads, blocks_here)
        (side,) = pack(
            table, [near], [[(chip, HANDED) for chip in range(chips)]], (tail,)
        )
        handed = core_swap(side)
        (main,) = pack(
            table, [near, handed], [[(chips + chip, MAIN) for chip in range(chips)]], ()
        )
        own_main = between_chips(main)
        (side,) = pack(
            table, [near], [[(2 * chips + chip, SECOND) for chip in range(chips)]], (main,)
        )
        handed = core_swap(side)
        token = (side,)
    for head in range(heads):
        if direct and head == 4:
            token = token + (loc, bounds, most)
        carry, token = local_head(
            head, gates, prev_ok, queries, keys, values, grad_out, halo, carry, token
        )
        if direct and head == 1:
            most = jnp.broadcast_to(jnp.pad(most, (0, 8 - chips))[:, None], (8, 128))
            most = most_of_all(most + token.astype(jnp.int32))
            hot = jnp.argmax(most[:chips, 0]).astype(jnp.int32)
            limit = jnp.where(jnp.arange(chips) == hot, 2 * SECOND, 0)
            overflow = jnp.any(most[:chips, 0] > limit)
            branch = jnp.where(overflow, chips, hot)
        token = (token,)

    def finish(start, stop, where, sources, made):
        return memory_heads(
            start, stop, where, gates, queries, grad_out, carry, sources, made
        )

    def full_exchange(halo_grad):
        returned, where = exchange_all(memory, block_ids)
        out, dq, _ = finish(0, jnp.array([0, heads], jnp.int32), where, [returned], ())
        return out, dq, passed_along(halo_grad, "tok", -1)

    back_k = passed_along(carry[6], "tok", -1)
    if not direct:
        out, dq, back_v = full_exchange(carry[7])
        return out, dq, *close_grads(carry, back_k, back_v, block_ids)

    def from_chip(source):
        def send(halo_grad):
            late = [chip_shift(seconds[(source + k) % chips], source, k) for k in range(1, chips)]
            back = passed_along(halo_grad, "tok", -1)
            sources = [near, own_main, core_swap(own_main)]
            *made, made_token = finish(0, bounds, loc, sources, ())
            late = summed(late, (made_token,))
            sources += [late, core_swap(late)]
            out, dq, _ = finish(1, bounds, loc, sources, made)
            return out, dq, back
        return send

    seconds = pack(
        table, [near, handed], [[(3 * chips + chip, SECOND)] for chip in range(chips)], token
    )
    own_main = held_back(own_main, seconds)
    out, dq, back_v = lax.switch(
        branch, [from_chip(source) for source in range(chips)] + [full_exchange], carry[7]
    )
    dk, dv = close_grads(carry, back_k, back_v, out)
    return out, dq, dk, dv


def solution(mesh):
    in_specs = (
        P("tok", "mem"),
        P("tok", "mem"),
        P("tok", "mem"),
        P("mem", "tok", None, None),
        P("tok", "mem", None),
        P("mem"),
        P("tok", "mem"),
    )
    out_specs = (P("tok", "mem"), P("tok", "mem"), P("tok", "mem"), P("tok", "mem"))
    return jax.shard_map(
        per_device, mesh=mesh, in_specs=in_specs, out_specs=out_specs, check_vma=False
    )
```
